32 devices in a mesh: row: 4 (over z), col: 8 (over y, x, core).
Axes of the slice: x: 2, y: 2, z: 4, core: 2. Of those that a mesh axis runs over, the one named last changes fastest.
Arguments:
- right_side: float32 [8, 16384], P(None, ('row', 'col')), may hold values from -30 to 30
- u_factors: bfloat16 [32, 64, 48, 512], P(('row', 'col')), may hold values from -0.109375 to 0.109375
- v_factors: bfloat16 [32, 64, 48, 512], P('row', 'col'), may hold values from -0.25 to 0.25
- ranks: int32 [32, 64], P('row', 'col'), may hold values from 8 to 48
- far_blocks: bfloat16 [8, 512, 32768], P('row', None, 'col'), may hold values from -0.09375 to 0.09375
- block_target: int32 [8, 8], replicated, may hold values from 0 to 31, as said below
- recv_order: int32 [32], replicated, may hold values from 0 to 31, as said below
Outputs:
- densities: float32 [8, 32768], P(None, 'col')
- residual: float32 [8, 16384], P(None, ('row', 'col'))
- far_field: float32 [32, 4096], P(('row', 'col'))
The draws below stay inside these ranges and needn't reach their ends.
Inputs may be any that keep to these rules, and one draw needn't show every extreme that they name: `recv_order`: a permutation of the receiver patches. `block_target`: block (b, c) with b % 2 == 0 lies on device g = (b // 2) * 8 + c; its receiver patch is stored in output rows owned by device (g + 32 / 2) mod 32 if g is even and by device g - 1 if g is odd; the other blocks may name any receiver patch.
All inputs are finite; a program needn't handle non-finite values.
Results may differ from the reference program's by a relative error of at most 0.008.
Values may be sent and summed in bfloat16 or wider, within the bound.
A program may use at most 128 MiB of HBM per device.

```python
import jax
import jax.numpy as jnp
from jax import lax

PATCH = 512
RMAX = 48
DENS = 8
CP_DEV = 8
FB_DEV = 2
RECV_DEV = 1
ITERS = 2
NP = 64
MP = 32
ORDER = 32768
FBR = 8
RECV = 32
N_COL = 8
DEVICES = 32


def draw_right_side(key, part):
    total_rows = MP * PATCH
    ramp = 1.0 + 2.0 * jnp.arange(total_rows, dtype=jnp.float32) / (total_rows - 1)
    values = jax.random.normal(key, (DENS, total_rows), jnp.float32)
    return jnp.clip(values, -8.0, 8.0) * ramp[None, :]


def shared_routing(key):
    perm_key = jax.random.fold_in(key, 11)
    return jax.random.permutation(perm_key, RECV).astype(jnp.int32)


def draw_recv_order(key, part):
    return shared_routing(key)


def draw_block_target(key, part):
    perm = shared_routing(key)
    slot_key = jax.random.fold_in(key, 23)
    first_key = jax.random.fold_in(key, 37)
    second_key = jax.random.fold_in(key, 41)
    block_rows = jnp.arange(FBR, dtype=jnp.int32)[:, None]
    col_index = jnp.arange(N_COL, dtype=jnp.int32)[None, :]
    device = block_rows // FB_DEV * N_COL + col_index
    within = block_rows % FB_DEV + 0 * col_index
    partner = jnp.where(device % 2 == 0, (device + DEVICES // 2) % DEVICES, device - 1)
    slot = jax.random.randint(slot_key, (FBR, N_COL), 0, RECV_DEV, dtype=jnp.int32)
    first_pos = partner * RECV_DEV + slot
    draw_one = jax.random.randint(first_key, (FBR, N_COL), 0, RECV, dtype=jnp.int32)
    draw_two = jax.random.randint(second_key, (FBR, N_COL), 0, RECV, dtype=jnp.int32)
    other_pos = jnp.minimum(draw_one, draw_two)
    position = jnp.where(within == 0, first_pos, other_pos).astype(jnp.int32)
    return perm[position]


def place_ends(array, stream_key, low, largest):
    dims = array.shape
    index_at = [jax.random.randint(jax.random.fold_in(stream_key, axis), (), 0, dims[axis]) for axis in range(len(dims))]
    array = array.at[tuple(index_at)].set(low)
    longest = dims.index(max(dims))
    index_at[longest] = (index_at[longest] + 1) % dims[longest]
    return array.at[tuple(index_at)].set(largest)


def block_scale(stream_key, shape, cuts, least, top_value):
    factor_of, own = 1.0, jax.random.fold_in(stream_key, 6)
    for axis_at, parts in cuts:
        draws = jnp.exp(jax.random.uniform(jax.random.fold_in(own, axis_at), (parts,), jnp.float32, least / len(cuts), top_value / len(cuts)))
        factor_of = factor_of * jnp.repeat(draws, shape[axis_at] // parts).reshape([-1 if axis == axis_at else 1 for axis in range(len(shape))])
    return factor_of


def normal_values(rng, shape, scale, limit, cuts=(), kind=jnp.bfloat16):
    values = scale * jax.random.normal(rng, shape, jnp.float32)
    if cuts:
        values = values * block_scale(rng, shape, cuts, -0.22, 0.18)
    return jnp.clip(values, -limit, limit).astype(kind)


def setup_inputs(seed: int = 0) -> dict:
    streams_of = jax.random.split(jax.random.key(seed), 8)
    return {
        "right_side": draw_right_side(jax.random.fold_in(streams_of[7], 71), 0),
        "u_factors": normal_values(streams_of[1], (MP, NP, RMAX, PATCH), (NP * RMAX) ** -0.5, 0.109375, ((0, 32),)),
        "v_factors": normal_values(streams_of[2], (MP, NP, RMAX, PATCH), PATCH ** -0.5, 0.25, ((0, 4), (1, 8))),
        "ranks": place_ends(jax.random.randint(streams_of[3], (MP, NP), RMAX // 6, RMAX + 1), jax.random.fold_in(streams_of[3], 1), RMAX // 6, RMAX).astype(jnp.int32),
        "far_blocks": normal_values(streams_of[4], (FBR, PATCH, ORDER), (CP_DEV * PATCH) ** -0.5, 0.09375, ((0, 4), (2, 8))),
        "block_target": draw_block_target(jax.random.fold_in(streams_of[7], 71), 0),
        "recv_order": draw_recv_order(jax.random.fold_in(streams_of[7], 71), 0),
    }


def reference(right_side, u_factors, v_factors, ranks, far_blocks, block_target, recv_order):
    slot_index = jnp.arange(RMAX, dtype=jnp.int32)
    kept = (slot_index[None, None, :, None] < ranks[:, :, None, None]).astype(jnp.float32)

    def adjoint(residual):
        res_bf = residual.astype(jnp.bfloat16).reshape(DENS, MP, PATCH).transpose(1, 0, 2)

        def accumulate(running, row_items):
            u_row, v_row, kept_row, res_row = row_items
            back_coef = jnp.einsum('jsp,dp->jsd', u_row.astype(jnp.float32), res_row.astype(jnp.float32))
            back_coef = back_coef.astype(jnp.bfloat16) * kept_row.astype(jnp.bfloat16)
            term = jnp.einsum('jsp,jsd->djp', v_row.astype(jnp.float32), back_coef.astype(jnp.float32))
            return running + term, None

        start_sum = jnp.zeros((DENS, NP, PATCH), jnp.float32)
        running, _ = lax.scan(accumulate, start_sum, (u_factors, v_factors, kept, res_bf))
        return running.reshape(DENS, NP * PATCH)

    def forward(grad):
        grad_bf = grad.astype(jnp.bfloat16).astype(jnp.float32).reshape(DENS, NP, PATCH)

        def one_row(row_items):
            u_row, v_row, kept_row = row_items
            coefficients = jnp.einsum('jsp,djp->jsd', v_row.astype(jnp.float32), grad_bf) * kept_row
            coefficients = coefficients.astype(jnp.bfloat16).astype(jnp.float32)
            return jnp.einsum('jsp,jsd->dp', u_row.astype(jnp.float32), coefficients)

        image = lax.map(one_row, (u_factors, v_factors, kept))
        return image.transpose(1, 0, 2).reshape(DENS, MP * PATCH)

    residual = right_side
    densities = jnp.zeros((DENS, NP * PATCH), jnp.float32)
    for iteration in range(ITERS):
        grad = adjoint(residual)
        grad_sq = jnp.sum(grad * grad, axis=1)
        image = forward(grad)
        image_sq = jnp.sum(image * image, axis=1)
        step_size = grad_sq / (image_sq + 1e-6)
        densities = densities + step_size[:, None] * grad
        residual = residual - step_size[:, None] * image

    x_groups = densities.astype(jnp.bfloat16).astype(jnp.float32).reshape(DENS, N_COL, CP_DEV * PATCH)

    def block_row(far_row):
        far_split = far_row.astype(jnp.float32).reshape(PATCH, N_COL, CP_DEV * PATCH)
        field = jnp.einsum('pcn,dcn->cdp', far_split, x_groups)
        return field.reshape(N_COL, DENS * PATCH)

    block_field = lax.map(block_row, far_blocks).reshape(FBR * N_COL, DENS * PATCH)
    onehot = (block_target.reshape(-1)[:, None] == recv_order[None, :]).astype(jnp.float32)
    far_field = jnp.dot(onehot.T, block_field, preferred_element_type=jnp.float32, precision=lax.Precision.HIGHEST)
    return densities, residual, far_field
```

```python
import functools

import jax
import jax.numpy as jnp
from jax import lax
from jax.experimental import pallas as pl
from jax.experimental.pallas import tpu as pltpu
from jax.sharding import PartitionSpec as P

MESH = pl.DeviceIdType.MESH
LANES = 128
NT = (((1,), (1,)), ((), ()))
NN = (((1,), (0,)), ((), ()))


def partner_of(me, k, n):
    if n & (n - 1):
        return (me + k) % n
    out = 0
    bit = 1
    while bit < n:
        mine = (me // bit) % 2
        out = out + bit * ((1 - mine) if k & bit else mine)
        bit *= 2
    return out


def sender_to(me, k, n):
    if n & (n - 1):
        return (me + n - k) % n
    return partner_of(me, k, n)


def kernel(
    nr, nc, dens_count, own_cols, slot_count, patch,
    rhs_ref, ranks_ref, target_ref, order_ref, u_hbm, v_hbm, f_hbm,
    dens_ref, resid_ref, far_ref,
    u_v, v_v, f_v, kept_ref, acc_ref, sum_ref,
    a2a_out, a2a_in, rs_out, rs_in, ag_buf, sc_col, sc_row, z_buf, fc_out, fc_in, ev_out, ev_in,
    u_sem, v_sem, f_sem, a2a_ss, a2a_rs, rs_ss, rs_rs, ag_ss, ag_rs,
    scc_ss, scc_rs, scr_ss, scr_rs, z_ss, z_rs, fc_ss, fc_rs, ev_ss, ev_rs,
):
    d = dens_count
    slots = own_cols * slot_count
    half = a2a_out.shape[-1]
    rows = own_cols * d
    chunk = rows // nr
    my_r = lax.axis_index("row")
    my_c = lax.axis_index("col")
    far_first = list(range(nc - 1, 0, -1))
    near_first = list(range(1, nc))
    row_first = list(range(nr - 1, 0, -1))
    bf = jnp.bfloat16
    f32 = jnp.float32

    u_copies = {}
    v_copies = {}
    for k in far_first + [0]:
        to = partner_of(my_c, k, nc)
        u_copies[k] = pltpu.make_async_copy(u_hbm.at[to], u_v.at[to], u_sem.at[k])
        u_copies[k].start()
    for k in [0] + near_first:
        frm = sender_to(my_c, k, nc)
        v_copies[k] = pltpu.make_async_copy(v_hbm.at[frm], v_v.at[frm], v_sem.at[k])
        v_copies[k].start()
    f_copies = []
    for b in range(2):
        f_copies.append(pltpu.make_async_copy(f_hbm.at[b], f_v.at[b], f_sem.at[b]))
        f_copies[b].start()

    barrier = pltpu.get_barrier_semaphore()
    for k in near_first:
        pl.semaphore_signal(
            barrier, inc=1, device_id=(my_r, partner_of(my_c, k, nc)), device_id_type=MESH
        )
    for k in row_first:
        pl.semaphore_signal(
            barrier, inc=1, device_id=(partner_of(my_r, k, nr), my_c), device_id_type=MESH
        )

    pending = []

    def send(src, dst, ssem, rsem, r, c):
        copy = pltpu.make_async_remote_copy(
            src_ref=src, dst_ref=dst, send_sem=ssem, recv_sem=rsem,
            device_id=(r, c), device_id_type=MESH,
        )
        copy.start()
        pending.append(copy)

    def arrive(src, dst, ssem, rsem):
        pltpu.make_async_remote_copy(
            src_ref=src, dst_ref=dst, send_sem=ssem, recv_sem=rsem,
            device_id=(my_r, my_c), device_id_type=MESH,
        ).wait_recv()

    def pack(x):
        top, low = x[:, :half], x[:, half:]
        if low.shape[1] < half:
            low = jnp.concatenate([low, jnp.zeros((d, half - low.shape[1]), f32)], axis=1)
        return jnp.concatenate([top, low], axis=0).astype(bf)

    def unpack(x):
        x = x.astype(f32)
        return jnp.concatenate([x[:d], x[d:, : slots - half]], axis=1)

    def post(rnd, to, k, value):
        if k == 0:
            a2a_in[rnd, my_c] = pack(value)
            return
        a2a_out[rnd, to] = pack(value)
        send(
            a2a_out.at[rnd, to], a2a_in.at[rnd, my_c], a2a_ss.at[rnd, to], a2a_rs.at[rnd, my_c],
            my_r, to,
        )

    def take(rnd, frm, k):
        if k:
            arrive(
                a2a_out.at[rnd, frm], a2a_in.at[rnd, frm], a2a_ss.at[rnd, frm],
                a2a_rs.at[rnd, frm],
            )
        return unpack(a2a_in[rnd, frm])

    lane_col = lax.broadcasted_iota(jnp.int32, (d, slots), 1) // slot_count
    diag = jnp.concatenate(
        [(lane_col == j).astype(f32) for j in range(own_cols)], axis=0
    )

    def back_pass(rnd, r, first):
        rb = r.astype(bf)
        for k in far_first + [0]:
            to = partner_of(my_c, k, nc)
            if first:
                u_copies[k].wait()
            value = lax.dot_general(rb, u_v[to], NT, preferred_element_type=f32)
            if first and k == far_first[0]:
                pl.semaphore_wait(barrier, nc - 1 + nr - 1)
            post(rnd, to, k, value)

    def grad_pass(rnd, first):
        acc = jnp.zeros((rows, patch), f32)
        for k in [0] + near_first:
            frm = sender_to(my_c, k, nc)
            if first:
                v_copies[k].wait()
            b = take(rnd, frm, k) * kept_ref[pl.ds(frm, 1), :]
            wide = (jnp.concatenate([b] * own_cols, axis=0) * diag).astype(bf)
            acc = acc + lax.dot_general(wide, v_v[frm], NN, preferred_element_type=f32)
        return acc

    def row_reduce(it, acc):
        acc_ref[...] = acc.reshape(nr, chunk, patch)
        for k in row_first:
            to = partner_of(my_r, k, nr)
            rs_out[it, to] = acc_ref[to].astype(rs_out.dtype)
            send(
                rs_out.at[it, to], rs_in.at[it, my_r], rs_ss.at[it, to], rs_rs.at[it, my_r],
                to, my_c,
            )
        total = acc_ref[my_r]
        for k in row_first[::-1]:
            frm = sender_to(my_r, k, nr)
            arrive(
                rs_out.at[it, frm], rs_in.at[it, frm], rs_ss.at[it, frm], rs_rs.at[it, frm]
            )
            total = total + rs_in[it, frm].astype(f32)
        return total

    def row_gather(it, g):
        ag_buf[it, my_r] = g.astype(ag_buf.dtype)
        for k in row_first:
            to = partner_of(my_r, k, nr)
            send(
                ag_buf.at[it, my_r], ag_buf.at[it, my_r], ag_ss.at[it, to], ag_rs.at[it, my_r],
                to, my_c,
            )
        for k in row_first[::-1]:
            frm = sender_to(my_r, k, nr)
            arrive(
                ag_buf.at[it, frm], ag_buf.at[it, frm], ag_ss.at[it, frm], ag_rs.at[it, frm]
            )
        return ag_buf[it].reshape(rows, patch).astype(bf)

    def coef_pass(rnd, g):
        for k in far_first + [0]:
            to = partner_of(my_c, k, nc)
            wide = lax.dot_general(g, v_v[to], NT, preferred_element_type=f32) * diag
            c = wide[:d]
            for j in range(1, own_cols):
                c = c + wide[j * d : (j + 1) * d]
            post(rnd, to, k, c * kept_ref[pl.ds(to, 1), :])

    def image_pass(rnd):
        image = jnp.zeros((d, patch), f32)
        for k in [0] + near_first:
            frm = sender_to(my_c, k, nc)
            c = take(rnd, frm, k).astype(bf)
            image = image + lax.dot_general(c, u_v[frm], NN, preferred_element_type=f32)
        return image

    lane = lax.broadcasted_iota(jnp.int32, (d, LANES), 1)

    def squares_out(it, g, image):
        grad_sq = jnp.zeros((d, 1), f32)
        for j in range(chunk // d):
            part = g[j * d : (j + 1) * d]
            grad_sq = grad_sq + jnp.sum(part * part, axis=1, keepdims=True)
        image_sq = jnp.sum(image * image, axis=1, keepdims=True)
        sc_col[it, my_c] = jnp.where(lane < LANES // 2, grad_sq, image_sq)
        for k in far_first:
            to = partner_of(my_c, k, nc)
            send(
                sc_col.at[it, my_c], sc_col.at[it, my_c], scc_ss.at[it, to],
                scc_rs.at[it, my_c], my_r, to,
            )

    def squares_on(it):
        for k in near_first:
            frm = sender_to(my_c, k, nc)
            arrive(
                sc_col.at[it, frm], sc_col.at[it, frm], scc_ss.at[it, frm], scc_rs.at[it, frm]
            )
        total = sc_col[it, 0]
        for c in range(1, nc):
            total = total + sc_col[it, c]
        sc_row[it, my_r] = total
        for k in row_first:
            to = partner_of(my_r, k, nr)
            send(
                sc_row.at[it, my_r], sc_row.at[it, my_r], scr_ss.at[it, to],
                scr_rs.at[it, my_r], to, my_c,
            )

    def squares_in(it):
        for k in row_first[::-1]:
            frm = sender_to(my_r, k, nr)
            arrive(
                sc_row.at[it, frm], sc_row.at[it, frm], scr_ss.at[it, frm], scr_rs.at[it, frm]
            )
        total = sc_row[it, 0]
        for r in range(1, nr):
            total = total + sc_row[it, r]
        return total[:, :1] / (total[:, LANES // 2 : LANES // 2 + 1] + 1e-6)

    rhs = rhs_ref[...]
    back_pass(0, rhs, True)
    lane_all = lax.broadcasted_iota(jnp.int32, (nc, slots), 1)
    ranks = ranks_ref[...]
    limit = jnp.zeros((nc, slots), jnp.int32)
    for j in range(own_cols):
        limit = jnp.where(lane_all // slot_count == j, ranks[:, j : j + 1], limit)
    kept_ref[...] = (lane_all % slot_count < limit).astype(f32)

    g1 = row_reduce(0, grad_pass(0, True))
    g1_all = row_gather(0, g1)
    coef_pass(1, g1_all)
    image1 = image_pass(1)
    back_pass(2, image1, False)
    squares_out(0, g1, image1)
    squares_on(0)
    h1 = row_reduce(1, grad_pass(2, False))
    step1 = squares_in(0)

    g2 = g1 - jnp.concatenate([step1] * (chunk // d), axis=0) * h1
    g2_all = row_gather(1, g2)
    coef_pass(3, g2_all)

    g1_wide = g1_all.astype(f32)
    g2_wide = g2_all.astype(f32)

    def field_of(b):
        f_copies[b].wait()
        field = jnp.zeros((2 * d, patch), f32)
        for j in range(own_cols):
            lhs = jnp.concatenate(
                [g1_wide[j * d : (j + 1) * d], g2_wide[j * d : (j + 1) * d]], axis=0
            ).astype(bf)
            field = field + lax.dot_general(
                lhs, f_v[b, :, j * patch : (j + 1) * patch], NT, preferred_element_type=f32
            )
        return field.astype(bf)

    z_buf[my_r] = field_of(1)
    for k in row_first:
        to = partner_of(my_r, k, nr)
        send(z_buf.at[my_r], z_buf.at[my_r], z_ss.at[to], z_rs.at[my_r], to, my_c)
    ev_out[...] = field_of(0)
    odd = my_c % 2
    ev_row = (1 - odd) * ((my_r + nr // 2) % nr) + odd * my_r
    ev_col = my_c - odd
    send(ev_out, ev_in.at[odd], ev_ss, ev_rs.at[odd], ev_row, ev_col)

    image2 = image_pass(3)
    squares_out(1, g2, image2)

    for k in row_first[::-1]:
        frm = sender_to(my_r, k, nr)
        arrive(z_buf.at[frm], z_buf.at[frm], z_ss.at[frm], z_rs.at[frm])
    fields = [z_buf[r].astype(f32) for r in range(nr)]
    targets = [target_ref[2 * r + 1, my_c] for r in range(nr)]
    for k in far_first + [0]:
        to = partner_of(my_c, k, nc)
        wanted = order_ref[my_r * nc + to]
        part = jnp.zeros((2 * d, patch), f32)
        for r in range(nr):
            part = part + fields[r] * jnp.where(targets[r] == wanted, 1.0, 0.0).astype(f32)
        if k:
            fc_out[to] = part.astype(bf)
            send(fc_out.at[to], fc_in.at[my_c], fc_ss.at[to], fc_rs.at[my_c], my_r, to)
        else:
            fc_in[my_c] = part.astype(bf)

    squares_on(1)
    for k in near_first:
        frm = sender_to(my_c, k, nc)
        arrive(fc_out.at[frm], fc_in.at[frm], fc_ss.at[frm], fc_rs.at[frm])
    got = fc_in[0].astype(f32)
    for c in range(1, nc):
        got = got + fc_in[c].astype(f32)

    sum_ref[...] = got

    @pl.when(odd == 0)
    def _():
        for s in range(2):
            arrive(ev_out, ev_in.at[s], ev_ss, ev_rs.at[s])
        sum_ref[...] = got + ev_in[0].astype(f32) + ev_in[1].astype(f32)

    field = sum_ref[...]
    step2 = squares_in(1)
    far = step1 * field[:d] + step2 * field[d:]
    for row in range(d):
        far_ref[:, row * patch : (row + 1) * patch] = far[row : row + 1]
    resid_ref[...] = rhs - step1 * image1 - step2 * image2
    for j in range(own_cols):
        dens_ref[:, j * patch : (j + 1) * patch] = (
            step1 * g1_wide[j * d : (j + 1) * d] + step2 * g2_wide[j * d : (j + 1) * d]
        )
    for copy in pending:
        copy.wait_send()


def per_device(nr, nc, right_side, u_factors, v_factors, ranks, far_blocks, block_target, recv_order):
    dens_count, patch = right_side.shape
    own_rows, all_cols, slot_count, _ = u_factors.shape
    group_rows, own_cols = v_factors.shape[:2]
    block_count, _, unknowns = far_blocks.shape
    recv_total = recv_order.shape[0]
    assert own_rows == 1 and group_rows == nc and all_cols == nc * own_cols
    assert block_count == 2 and recv_total == nr * nc and unknowns == own_cols * patch
    slots = own_cols * slot_count
    rows = own_cols * dens_count
    chunk = rows // nr
    half = -(-slots // (2 * LANES)) * LANES
    bf = jnp.bfloat16
    f32 = jnp.float32
    wire = bf if chunk % 16 == 0 else f32
    dma = pltpu.SemaphoreType.DMA
    u = u_factors.reshape(nc, slots, patch)
    v = v_factors.reshape(group_rows, slots, patch)
    vmem = pl.BlockSpec(memory_space=pltpu.VMEM)
    smem = pl.BlockSpec(memory_space=pltpu.SMEM)
    hbm = pl.BlockSpec(memory_space=pl.ANY)
    scratch = [
        pltpu.VMEM(u.shape, bf),
        pltpu.VMEM(v.shape, bf),
        pltpu.VMEM(far_blocks.shape, bf),
        pltpu.VMEM((nc, slots), f32),
        pltpu.VMEM((nr, chunk, patch), f32),
        pltpu.VMEM((2 * dens_count, patch), f32),
        pltpu.VMEM((4, nc, 2 * dens_count, half), bf),
        pltpu.VMEM((4, nc, 2 * dens_count, half), bf),
        pltpu.VMEM((2, nr, chunk, patch), wire),
        pltpu.VMEM((2, nr, chunk, patch), wire),
        pltpu.VMEM((2, nr, chunk, patch), wire),
        pltpu.VMEM((2, nc, dens_count, LANES), f32),
        pltpu.VMEM((2, nr, dens_count, LANES), f32),
        pltpu.VMEM((nr, 2 * dens_count, patch), bf),
        pltpu.VMEM((nc, 2 * dens_count, patch), bf),
        pltpu.VMEM((nc, 2 * dens_count, patch), bf),
        pltpu.VMEM((2 * dens_count, patch), bf),
        pltpu.VMEM((2, 2 * dens_count, patch), bf),
        dma((nc,)), dma((nc,)), dma((2,)),
        dma((4, nc)), dma((4, nc)),
        dma((2, nr)), dma((2, nr)),
        dma((2, nr)), dma((2, nr)),
        dma((2, nc)), dma((2, nc)),
        dma((2, nr)), dma((2, nr)),
        dma((nr,)), dma((nr,)),
        dma((nc,)), dma((nc,)),
        dma, dma((2,)),
    ]
    matrix = u.size + v.size
    return pl.pallas_call(
        functools.partial(kernel, nr, nc, dens_count, own_cols, slot_count, patch),
        out_shape=(
            jax.ShapeDtypeStruct((dens_count, unknowns), f32),
            jax.ShapeDtypeStruct((dens_count, patch), f32),
            jax.ShapeDtypeStruct((1, dens_count * patch), f32),
        ),
        in_specs=[vmem, vmem, smem, smem, hbm, hbm, hbm],
        out_specs=(vmem, vmem, vmem),
        scratch_shapes=scratch,
        compiler_params=pltpu.CompilerParams(
            collective_id=0, has_side_effects=True, vmem_limit_bytes=56 * 1024 * 1024
        ),
        cost_estimate=pl.CostEstimate(
            flops=8 * dens_count * matrix + 2 * dens_count * far_blocks.size,
            bytes_accessed=2 * (matrix + far_blocks.size), transcendentals=0,
        ),
    )(right_side, ranks, block_target, recv_order, u, v, far_blocks)


def solution(mesh):
    return jax.shard_map(
        functools.partial(per_device, mesh.shape["row"], mesh.shape["col"]),
        mesh=mesh,
        in_specs=(
            P(None, ("row", "col")),
            P(("row", "col"), None, None, None),
            P("row", "col", None, None),
            P("row", "col"),
            P("row", None, "col"),
            P(),
            P(),
        ),
        out_specs=(P(None, "col"), P(None, ("row", "col")), P(("row", "col"), None)),
        check_vma=False,
    )
```

```python
import functools

import jax
import jax.numpy as jnp
from jax import lax
from jax.experimental import pallas as pl
from jax.experimental.pallas import tpu as pltpu
from jax.sharding import PartitionSpec as P

MESH = pl.DeviceIdType.MESH
LANES = 128
NT = (((1,), (1,)), ((), ()))
NN = (((1,), (0,)), ((), ()))


def partner_of(me, k, n):
    if n & (n - 1):
        return (me + k) % n
    out = 0
    bit = 1
    while bit < n:
        mine = (me // bit) % 2
        out = out + bit * ((1 - mine) if k & bit else mine)
        bit *= 2
    return out


def kernel(
    nr, nc, dens_count, own_cols, slot_count, patch,
    rhs_ref, ranks_ref, target_ref, order_ref, u_hbm, v_hbm, f_hbm,
    dens_ref, resid_ref, far_ref,
    u_v, v_v, f_v, kept_ref, acc_ref, sum_ref,
    a2a_out, a2a_in, rs_out, rs_in, ag_buf, sc_col, sc_row, z_buf, fc_out, fc_in, ev_out, ev_in,
    load_sem, a2a_ss, a2a_rs, rs_ss, rs_rs, ag_ss, ag_rs,
    scc_ss, scc_rs, scr_ss, scr_rs, z_ss, z_rs, fc_ss, fc_rs, ev_ss, ev_rs,
):
    d = dens_count
    slots = own_cols * slot_count
    half = a2a_out.shape[-1]
    rows = own_cols * d
    chunk = rows // nr
    my_r = lax.axis_index("row")
    my_c = lax.axis_index("col")
    col_peers = [partner_of(my_c, k, nc) for k in range(nc - 1, 0, -1)]
    row_peers = [partner_of(my_r, k, nr) for k in range(nr - 1, 0, -1)]
    bf = jnp.bfloat16
    f32 = jnp.float32

    u_copy = pltpu.make_async_copy(u_hbm, u_v, load_sem.at[0])
    v_copy = pltpu.make_async_copy(v_hbm, v_v, load_sem.at[1])
    f_copies = [pltpu.make_async_copy(f_hbm.at[b], f_v.at[b], load_sem.at[2 + b]) for b in range(2)]
    u_copy.start()

    barrier = pltpu.get_barrier_semaphore()
    for to in col_peers:
        pl.semaphore_signal(barrier, inc=1, device_id=(my_r, to), device_id_type=MESH)
    for to in row_peers:
        pl.semaphore_signal(barrier, inc=1, device_id=(to, my_c), device_id_type=MESH)

    def remote(src, dst, ssem, rsem, r, c):
        return pltpu.make_async_remote_copy(
            src_ref=src, dst_ref=dst, send_sem=ssem, recv_sem=rsem,
            device_id=(r, c), device_id_type=MESH,
        )

    def over_col(out, into, ssem, rsem, shared=False):
        for to in col_peers:
            src = out.at[my_c] if shared else out.at[to]
            remote(src, into.at[my_c], ssem, rsem, my_r, to).start()
        return remote(out.at[: nc - 1], into.at[: nc - 1], ssem, rsem, my_r, my_c)

    def over_row(out, into, ssem, rsem, shared=False):
        for to in row_peers:
            src = out.at[my_r] if shared else out.at[to]
            remote(src, into.at[my_r], ssem, rsem, to, my_c).start()
        return remote(out.at[: nr - 1], into.at[: nr - 1], ssem, rsem, my_r, my_c)

    def pack(x):
        top, low = x[:, :half], x[:, half:]
        if low.shape[1] < half:
            low = jnp.concatenate([low, jnp.zeros((d, half - low.shape[1]), f32)], axis=1)
        return jnp.concatenate([top, low], axis=0).astype(bf)

    def unpack(x):
        x = x.astype(f32)
        return jnp.concatenate([x[:d], x[d:, : slots - half]], axis=1)

    def exchange(rnd, values):
        for c in range(nc):
            a2a_out[rnd, c] = pack(values[c])
        sent = over_col(a2a_out.at[rnd], a2a_in.at[rnd], a2a_ss.at[rnd], a2a_rs.at[rnd])
        a2a_in[rnd, my_c] = a2a_out[rnd, my_c]
        return sent

    lane_col = lax.broadcasted_iota(jnp.int32, (d, slots), 1) // slot_count
    diag = jnp.concatenate([(lane_col == j).astype(f32) for j in range(own_cols)], axis=0)

    def back_of(r):
        rb = r.astype(bf)
        return [
            lax.dot_general(rb, u_v[c], NT, preferred_element_type=f32) for c in range(nc)
        ]

    def grad_of(rnd):
        acc = jnp.zeros((rows, patch), f32)
        for c in range(nc):
            b = unpack(a2a_in[rnd, c]) * kept_ref[c : c + 1, :]
            wide = (jnp.concatenate([b] * own_cols, axis=0) * diag).astype(bf)
            acc = acc + lax.dot_general(wide, v_v[c], NN, preferred_element_type=f32)
        return acc.reshape(nr, chunk, patch)

    def reduce_start(it, acc):
        rs_out[it] = acc.astype(rs_out.dtype)
        sent = over_row(rs_out.at[it], rs_in.at[it], rs_ss.at[it], rs_rs.at[it])
        acc_ref[...] = acc
        rs_in[it, my_r] = jnp.zeros((chunk, patch), rs_in.dtype)
        return sent

    def reduce_end(it, sent):
        total = acc_ref[my_r]
        sent.wait_recv()
        for r in range(nr):
            total = total + rs_in[it, r].astype(f32)
        return total

    def gather_start(it, g):
        ag_buf[it, my_r] = g.astype(ag_buf.dtype)
        return over_row(ag_buf.at[it], ag_buf.at[it], ag_ss.at[it], ag_rs.at[it], shared=True)

    def gathered(it):
        return ag_buf[it].reshape(rows, patch).astype(bf)

    def coef_of(g):
        values = []
        for c in range(nc):
            wide = lax.dot_general(g, v_v[c], NT, preferred_element_type=f32) * diag
            part = wide[:d]
            for j in range(1, own_cols):
                part = part + wide[j * d : (j + 1) * d]
            values.append(part * kept_ref[c : c + 1, :])
        return values

    def image_of(rnd):
        image = jnp.zeros((d, patch), f32)
        for c in range(nc):
            coef = unpack(a2a_in[rnd, c]).astype(bf)
            image = image + lax.dot_general(coef, u_v[c], NN, preferred_element_type=f32)
        return image

    lane = lax.broadcasted_iota(jnp.int32, (d, LANES), 1)

    def squares_out(it, g, image):
        squares = jnp.zeros((d, patch), f32)
        for j in range(chunk // d):
            squares = squares + g[j * d : (j + 1) * d] * g[j * d : (j + 1) * d]
        grad_sq = jnp.sum(squares, axis=1, keepdims=True)
        image_sq = jnp.sum(image * image, axis=1, keepdims=True)
        sc_col[it, my_c] = jnp.where(lane < LANES // 2, grad_sq, image_sq)
        return over_col(
            sc_col.at[it], sc_col.at[it], scc_ss.at[it], scc_rs.at[it], shared=True
        )

    def squares_on(it, sent):
        sent.wait_recv()
        total = sc_col[it, 0]
        for c in range(1, nc):
            total = total + sc_col[it, c]
        sc_row[it, my_r] = total
        return over_row(
            sc_row.at[it], sc_row.at[it], scr_ss.at[it], scr_rs.at[it], shared=True
        )

    def squares_in(it, sent):
        sent.wait_recv()
        total = sc_row[it, 0]
        for r in range(1, nr):
            total = total + sc_row[it, r]
        return total[:, :1] / (total[:, LANES // 2 : LANES // 2 + 1] + 1e-6)

    rhs = rhs_ref[...]
    lane_all = lax.broadcasted_iota(jnp.int32, (nc, slots), 1)
    ranks = ranks_ref[...]
    limit = jnp.zeros((nc, slots), jnp.int32)
    for j in range(own_cols):
        limit = jnp.where(lane_all // slot_count == j, ranks[:, j : j + 1], limit)
    kept_ref[...] = (lane_all % slot_count < limit).astype(f32)
    u_copy.wait()
    v_copy.start()
    back0 = back_of(rhs)
    pl.semaphore_wait(barrier, nc - 1 + nr - 1)
    x0 = exchange(0, back0)
    v_copy.wait()
    for copy in f_copies[::-1]:
        copy.start()
    x0.wait_recv()
    s0 = reduce_start(0, grad_of(0))
    x0.wait_send()
    g1 = reduce_end(0, s0)
    a0 = gather_start(0, g1)
    s0.wait_send()
    a0.wait_recv()
    g1_all = gathered(0)
    x1 = exchange(1, coef_of(g1_all))
    a0.wait_send()
    x1.wait_recv()
    image1 = image_of(1)
    x2 = exchange(2, back_of(image1))
    q0 = squares_out(0, g1, image1)
    x1.wait_send()
    x2.wait_recv()
    s1 = reduce_start(1, grad_of(2))
    p0 = squares_on(0, q0)
    x2.wait_send()
    h1 = reduce_end(1, s1)
    step1 = squares_in(0, p0)

    g2 = g1 - jnp.concatenate([step1] * (chunk // d), axis=0) * h1
    a1 = gather_start(1, g2)
    s1.wait_send()
    q0.wait_send()
    p0.wait_send()
    a1.wait_recv()
    g2_all = gathered(1)
    x3 = exchange(3, coef_of(g2_all))

    g1_wide = g1_all.astype(f32)
    g2_wide = g2_all.astype(f32)

    def field_of(b):
        field = jnp.zeros((2 * d, patch), f32)
        for j in range(own_cols):
            lhs = jnp.concatenate(
                [g1_wide[j * d : (j + 1) * d], g2_wide[j * d : (j + 1) * d]], axis=0
            ).astype(bf)
            field = field + lax.dot_general(
                lhs, f_v[b, :, j * patch : (j + 1) * patch], NT, preferred_element_type=f32
            )
        return field.astype(bf)

    for copy in f_copies:
        copy.wait()
    z_buf[my_r] = field_of(1)
    z = over_row(z_buf, z_buf, z_ss, z_rs, shared=True)
    x3.wait_recv()
    image2 = image_of(3)
    q1 = squares_out(1, g2, image2)

    ev_out[...] = field_of(0)
    odd = my_c % 2
    ev_row = (1 - odd) * ((my_r + nr // 2) % nr) + odd * my_r
    ev = remote(ev_out, ev_in.at[odd], ev_ss, ev_rs.at[odd], ev_row, my_c - odd)
    ev.start()
    p1 = squares_on(1, q1)

    z.wait_recv()
    fields = [z_buf[r].astype(f32) for r in range(nr)]
    targets = [target_ref[2 * r + 1, my_c] for r in range(nr)]
    for to in range(nc):
        wanted = order_ref[my_r * nc + to]
        part = jnp.zeros((2 * d, patch), f32)
        for r in range(nr):
            part = part + fields[r] * jnp.where(targets[r] == wanted, 1.0, 0.0).astype(f32)
        fc_out[to] = part.astype(bf)
    fc = over_col(fc_out, fc_in, fc_ss, fc_rs)
    fc_in[my_c] = fc_out[my_c]
    x3.wait_send()
    a1.wait_send()
    z.wait_send()
    q1.wait_send()
    step2 = squares_in(1, p1)
    resid_ref[...] = rhs - step1 * image1 - step2 * image2
    for j in range(own_cols):
        dens_ref[:, j * patch : (j + 1) * patch] = (
            step1 * g1_wide[j * d : (j + 1) * d] + step2 * g2_wide[j * d : (j + 1) * d]
        )
    sum_ref[...] = jnp.zeros((2 * d, patch), f32)

    @pl.when(odd == 0)
    def _():
        for s in range(2):
            remote(ev_out, ev_in.at[s], ev_ss, ev_rs.at[s], my_r, my_c).wait_recv()
        sum_ref[...] = ev_in[0].astype(f32) + ev_in[1].astype(f32)

    fc.wait_recv()
    field = sum_ref[...]
    for c in range(nc):
        field = field + fc_in[c].astype(f32)
    far = step1 * field[:d] + step2 * field[d:]
    for row in range(d):
        far_ref[:, row * patch : (row + 1) * patch] = far[row : row + 1]
    ev.wait_send()
    p1.wait_send()
    fc.wait_send()


def hand_on(*refs):
    count = len(refs) // 2
    sems = refs[-1]
    copies = [
        pltpu.make_async_copy(refs[n], refs[count + n], sems.at[n]) for n in range(count)
    ]
    for copy in copies:
        copy.start()
    for copy in copies:
        copy.wait()


def per_device(nr, nc, right_side, u_factors, v_factors, ranks, far_blocks, block_target, recv_order):
    dens_count, patch = right_side.shape
    own_rows, all_cols, slot_count, _ = u_factors.shape
    group_rows, own_cols = v_factors.shape[:2]
    block_count, _, unknowns = far_blocks.shape
    recv_total = recv_order.shape[0]
    assert own_rows == 1 and group_rows == nc and all_cols == nc * own_cols
    assert block_count == 2 and recv_total == nr * nc and unknowns == own_cols * patch
    slots = own_cols * slot_count
    rows = own_cols * dens_count
    chunk = rows // nr
    half = -(-slots // (2 * LANES)) * LANES
    bf = jnp.bfloat16
    f32 = jnp.float32
    wire = bf if chunk % 16 == 0 else f32
    dma = pltpu.SemaphoreType.DMA
    u = u_factors.reshape(nc, slots, patch)
    v = v_factors.reshape(group_rows, slots, patch)
    vmem = pl.BlockSpec(memory_space=pltpu.VMEM)
    smem = pl.BlockSpec(memory_space=pltpu.SMEM)
    hbm = pl.BlockSpec(memory_space=pl.ANY)
    scratch = [
        pltpu.VMEM(u.shape, bf),
        pltpu.VMEM(v.shape, bf),
        pltpu.VMEM(far_blocks.shape, bf),
        pltpu.VMEM((nc, slots), f32),
        pltpu.VMEM((nr, chunk, patch), f32),
        pltpu.VMEM((2 * dens_count, patch), f32),
        pltpu.VMEM((4, nc, 2 * dens_count, half), bf),
        pltpu.VMEM((4, nc, 2 * dens_count, half), bf),
        pltpu.VMEM((2, nr, chunk, patch), wire),
        pltpu.VMEM((2, nr, chunk, patch), wire),
        pltpu.VMEM((2, nr, chunk, patch), wire),
        pltpu.VMEM((2, nc, dens_count, LANES), f32),
        pltpu.VMEM((2, nr, dens_count, LANES), f32),
        pltpu.VMEM((nr, 2 * dens_count, patch), bf),
        pltpu.VMEM((nc, 2 * dens_count, patch), bf),
        pltpu.VMEM((nc, 2 * dens_count, patch), bf),
        pltpu.VMEM((2 * dens_count, patch), bf),
        pltpu.VMEM((2, 2 * dens_count, patch), bf),
        dma((4,)),
        dma((4,)), dma((4,)),
        dma((2,)), dma((2,)),
        dma((2,)), dma((2,)),
        dma((2,)), dma((2,)),
        dma((2,)), dma((2,)),
        dma, dma,
        dma, dma,
        dma, dma((2,)),
    ]
    matrix = u.size + v.size
    results = pl.pallas_call(
        functools.partial(kernel, nr, nc, dens_count, own_cols, slot_count, patch),
        out_shape=(
            jax.ShapeDtypeStruct((dens_count, unknowns), f32),
            jax.ShapeDtypeStruct((dens_count, patch), f32),
            jax.ShapeDtypeStruct((1, dens_count * patch), f32),
        ),
        in_specs=[vmem, vmem, smem, smem, hbm, hbm, hbm],
        out_specs=(vmem, vmem, vmem),
        scratch_shapes=scratch,
        compiler_params=pltpu.CompilerParams(
            collective_id=0, has_side_effects=True, vmem_limit_bytes=56 * 1024 * 1024
        ),
        cost_estimate=pl.CostEstimate(
            flops=8 * dens_count * matrix + 2 * dens_count * far_blocks.size,
            bytes_accessed=2 * (matrix + far_blocks.size), transcendentals=0,
        ),
    )(right_side, ranks, block_target, recv_order, u, v, far_blocks)
    return pl.pallas_call(
        hand_on,
        out_shape=tuple(jax.ShapeDtypeStruct(x.shape, x.dtype) for x in results),
        in_specs=[pl.BlockSpec(memory_space=pltpu.HBM)] * len(results),
        out_specs=(pl.BlockSpec(memory_space=pltpu.HBM),) * len(results),
        scratch_shapes=[dma((len(results),))],
    )(*results)


def solution(mesh):
    return jax.shard_map(
        functools.partial(per_device, mesh.shape["row"], mesh.shape["col"]),
        mesh=mesh,
        in_specs=(
            P(None, ("row", "col")),
            P(("row", "col"), None, None, None),
            P("row", "col", None, None),
            P("row", "col"),
            P("row", None, "col"),
            P(),
            P(),
        ),
        out_specs=(P(None, "col"), P(None, ("row", "col")), P(("row", "col"), None)),
        check_vma=False,
    )
```

```python
import functools

import jax
import jax.numpy as jnp
from jax import lax
from jax.experimental import pallas as pl
from jax.experimental.pallas import tpu as pltpu
from jax.sharding import PartitionSpec as P

MESH = pl.DeviceIdType.MESH
LANES = 128
NT = (((1,), (1,)), ((), ()))
NN = (((1,), (0,)), ((), ()))


def partner_of(me, k, n):
    if n & (n - 1):
        return (me + k) % n
    out = 0
    bit = 1
    while bit < n:
        mine = (me // bit) % 2
        out = out + bit * ((1 - mine) if k & bit else mine)
        bit *= 2
    return out


def kernel(
    nr, nc, dens_count, own_cols, slot_count, patch, pair,
    rhs_ref, ranks_ref, target_ref, order_ref, u_hbm, v_hbm, f_hbm,
    dens_ref, resid_ref, far_ref,
    u_v, v_v, f_v, x_v, kept_ref, acc_ref, sum_ref,
    a2a_out, a2a_in, rs_out, rs_in, ag_buf, sc_col, sc_row, z_buf, fc_out, fc_in, ev_out, ev_in,
    load_sem, a2a_ss, a2a_rs, rs_ss, rs_rs, ag_ss, ag_rs,
    scc_ss, scc_rs, scr_ss, scr_rs, z_ss, z_rs, fc_ss, fc_rs, ev_ss, ev_rs,
):
    d = dens_count
    slots = own_cols * slot_count
    half = a2a_out.shape[-1]
    rows = own_cols * d
    chunk = rows // nr
    my_r = lax.axis_index("row")
    my_c = lax.axis_index("col")
    col_peers = [partner_of(my_c, k, nc) for k in range(nc - 1, 0, -1)]
    row_peers = [partner_of(my_r, k, nr) for k in range(nr - 1, 0, -1)]
    bf = jnp.bfloat16
    f32 = jnp.float32

    u_copy = pltpu.make_async_copy(u_hbm, u_v, load_sem.at[0])
    v_copy = pltpu.make_async_copy(v_hbm, v_v, load_sem.at[1])
    f_copies = [pltpu.make_async_copy(f_hbm.at[b], f_v.at[b], load_sem.at[2 + b]) for b in range(2)]
    u_copy.start()

    barrier = pltpu.get_barrier_semaphore()
    for to in col_peers:
        pl.semaphore_signal(barrier, inc=1, device_id=(my_r, to), device_id_type=MESH)
    for to in row_peers:
        pl.semaphore_signal(barrier, inc=1, device_id=(to, my_c), device_id_type=MESH)

    def remote(src, dst, ssem, rsem, r, c):
        return pltpu.make_async_remote_copy(
            src_ref=src, dst_ref=dst, send_sem=ssem, recv_sem=rsem,
            device_id=(r, c), device_id_type=MESH,
        )

    def over_col(out, into, ssem, rsem, shared=False):
        for to in col_peers:
            src = out.at[my_c] if shared else out.at[to]
            remote(src, into.at[my_c], ssem, rsem, my_r, to).start()
        return remote(out.at[: nc - 1], into.at[: nc - 1], ssem, rsem, my_r, my_c)

    def over_row(out, into, ssem, rsem, shared=False):
        for to in row_peers:
            src = out.at[my_r] if shared else out.at[to]
            remote(src, into.at[my_r], ssem, rsem, to, my_c).start()
        return remote(out.at[: nr - 1], into.at[: nr - 1], ssem, rsem, my_r, my_c)

    def pack(x):
        top, low = x[:, :half], x[:, half:]
        if low.shape[1] < half:
            low = jnp.concatenate([low, jnp.zeros((d, half - low.shape[1]), f32)], axis=1)
        return jnp.concatenate([top, low], axis=0).astype(bf)

    def unpack(x):
        x = x.astype(f32)
        return jnp.concatenate([x[:d], x[d:, : slots - half]], axis=1)

    wide = pair * slots
    lane_col = lax.broadcasted_iota(jnp.int32, (d, wide), 1) % slots // slot_count
    diag = jnp.concatenate([(lane_col == j).astype(f32) for j in range(own_cols)], axis=0)

    def group(ref, q):
        return ref[pl.ds(pl.multiple_of(q * wide, wide), wide), :]

    def put(rnd, q, value):
        for n in range(pair):
            a2a_out[rnd, q * pair + n] = pack(value[:, n * slots : (n + 1) * slots])

    def got(rnd, q):
        return jnp.concatenate([unpack(a2a_in[rnd, q * pair + n]) for n in range(pair)], axis=1)

    def exchange(rnd):
        sent = over_col(a2a_out.at[rnd], a2a_in.at[rnd], a2a_ss.at[rnd], a2a_rs.at[rnd])
        a2a_in[rnd, my_c] = a2a_out[rnd, my_c]
        return sent

    def back_of(rnd, r):
        rb = r.astype(bf)

        def body(q, _):
            put(rnd, q, lax.dot_general(rb, group(u_v, q), NT, preferred_element_type=f32))
            return _

        lax.fori_loop(0, nc // pair, body, 0, unroll=2)

    def grad_of(rnd):
        def body(q, acc):
            b = got(rnd, q) * kept_ref[pl.ds(q, 1), :]
            spread = (jnp.concatenate([b] * own_cols, axis=0) * diag).astype(bf)
            return acc + lax.dot_general(spread, group(v_v, q), NN, preferred_element_type=f32)

        acc = lax.fori_loop(
            0, nc // pair, body, jnp.zeros((rows, patch), f32), unroll=2
        )
        return acc.reshape(nr, chunk, patch)

    def reduce_start(it, acc):
        rs_out[it] = acc.astype(rs_out.dtype)
        sent = over_row(rs_out.at[it], rs_in.at[it], rs_ss.at[it], rs_rs.at[it])
        acc_ref[...] = acc
        rs_in[it, my_r] = jnp.zeros((chunk, patch), rs_in.dtype)
        return sent

    def reduce_end(it, sent):
        total = acc_ref[my_r]
        sent.wait_recv()
        for r in range(nr):
            total = total + rs_in[it, r].astype(f32)
        return total

    def gather_start(it, g):
        ag_buf[it, my_r] = g.astype(ag_buf.dtype)
        return over_row(ag_buf.at[it], ag_buf.at[it], ag_ss.at[it], ag_rs.at[it], shared=True)

    def gathered(it):
        return ag_buf[it].reshape(rows, patch).astype(bf)

    def coef_of(rnd, g):
        def body(q, _):
            full = lax.dot_general(g, group(v_v, q), NT, preferred_element_type=f32) * diag
            part = full[:d]
            for j in range(1, own_cols):
                part = part + full[j * d : (j + 1) * d]
            put(rnd, q, part * kept_ref[pl.ds(q, 1), :])
            return _

        lax.fori_loop(0, nc // pair, body, 0, unroll=2)

    def image_of(rnd):
        def body(q, image):
            coef = got(rnd, q).astype(bf)
            return image + lax.dot_general(coef, group(u_v, q), NN, preferred_element_type=f32)

        return lax.fori_loop(0, nc // pair, body, jnp.zeros((d, patch), f32), unroll=2)

    lane = lax.broadcasted_iota(jnp.int32, (d, LANES), 1)

    def squares_out(it, g, image):
        squares = jnp.zeros((d, patch), f32)
        for j in range(chunk // d):
            squares = squares + g[j * d : (j + 1) * d] * g[j * d : (j + 1) * d]
        grad_sq = jnp.sum(squares, axis=1, keepdims=True)
        image_sq = jnp.sum(image * image, axis=1, keepdims=True)
        sc_col[it, my_c] = jnp.where(lane < LANES // 2, grad_sq, image_sq)
        return over_col(
            sc_col.at[it], sc_col.at[it], scc_ss.at[it], scc_rs.at[it], shared=True
        )

    def squares_on(it, sent):
        sent.wait_recv()
        total = sc_col[it, 0]
        for c in range(1, nc):
            total = total + sc_col[it, c]
        sc_row[it, my_r] = total
        return over_row(
            sc_row.at[it], sc_row.at[it], scr_ss.at[it], scr_rs.at[it], shared=True
        )

    def squares_in(it, sent):
        sent.wait_recv()
        total = sc_row[it, 0]
        for r in range(1, nr):
            total = total + sc_row[it, r]
        return total[:, :1] / (total[:, LANES // 2 : LANES // 2 + 1] + 1e-6)

    rhs = rhs_ref[...]
    lane_all = lax.broadcasted_iota(jnp.int32, (nc, slots), 1)
    ranks = ranks_ref[...]
    limit = jnp.zeros((nc, slots), jnp.int32)
    for j in range(own_cols):
        limit = jnp.where(lane_all // slot_count == j, ranks[:, j : j + 1], limit)
    kept = (lane_all % slot_count < limit).astype(f32)
    for c in range(nc):
        kept_ref[c // pair : c // pair + 1, pl.ds(c % pair * slots, slots)] = kept[c : c + 1]
    u_copy.wait()
    v_copy.start()
    back_of(0, rhs)
    pl.semaphore_wait(barrier, nc - 1 + nr - 1)
    x0 = exchange(0)
    v_copy.wait()
    for copy in f_copies[::-1]:
        copy.start()
    x0.wait_recv()
    s0 = reduce_start(0, grad_of(0))
    x0.wait_send()
    g1 = reduce_end(0, s0)
    a0 = gather_start(0, g1)
    s0.wait_send()
    a0.wait_recv()
    g1_all = gathered(0)
    coef_of(1, g1_all)
    x1 = exchange(1)
    a0.wait_send()
    x1.wait_recv()
    image1 = image_of(1)
    back_of(2, image1)
    x2 = exchange(2)
    q0 = squares_out(0, g1, image1)
    x1.wait_send()
    x2.wait_recv()
    s1 = reduce_start(1, grad_of(2))
    p0 = squares_on(0, q0)
    x2.wait_send()
    h1 = reduce_end(1, s1)
    step1 = squares_in(0, p0)

    g2 = g1 - jnp.concatenate([step1] * (chunk // d), axis=0) * h1
    a1 = gather_start(1, g2)
    s1.wait_send()
    q0.wait_send()
    p0.wait_send()
    a1.wait_recv()
    g2_all = gathered(1)
    coef_of(3, g2_all)
    x3 = exchange(3)

    g1_wide = g1_all.astype(f32)
    g2_wide = g2_all.astype(f32)

    for j in range(own_cols):
        x_v[:, j * patch : (j + 1) * patch] = jnp.concatenate(
            [g1_wide[j * d : (j + 1) * d], g2_wide[j * d : (j + 1) * d]], axis=0
        ).astype(bf)

    def field_of(b):
        def body(j, field):
            at = pl.ds(pl.multiple_of(j * patch, patch), patch)
            return field + lax.dot_general(
                x_v[:, at], f_v[b, :, at], NT, preferred_element_type=f32
            )

        start = jnp.zeros((2 * d, patch), f32)
        return lax.fori_loop(0, own_cols, body, start, unroll=2).astype(bf)

    for copy in f_copies:
        copy.wait()
    z_buf[my_r] = field_of(1)
    z = over_row(z_buf, z_buf, z_ss, z_rs, shared=True)
    x3.wait_recv()
    image2 = image_of(3)
    q1 = squares_out(1, g2, image2)

    ev_out[...] = field_of(0)
    odd = my_c % 2
    ev_row = (1 - odd) * ((my_r + nr // 2) % nr) + odd * my_r
    ev = remote(ev_out, ev_in.at[odd], ev_ss, ev_rs.at[odd], ev_row, my_c - odd)
    ev.start()
    p1 = squares_on(1, q1)

    z.wait_recv()
    fields = [z_buf[r].astype(f32) for r in range(nr)]
    targets = [target_ref[2 * r + 1, my_c] for r in range(nr)]
    for to in range(nc):
        wanted = order_ref[my_r * nc + to]
        part = jnp.zeros((2 * d, patch), f32)
        for r in range(nr):
            part = part + fields[r] * jnp.where(targets[r] == wanted, 1.0, 0.0).astype(f32)
        fc_out[to] = part.astype(bf)
    fc = over_col(fc_out, fc_in, fc_ss, fc_rs)
    fc_in[my_c] = fc_out[my_c]
    x3.wait_send()
    a1.wait_send()
    z.wait_send()
    q1.wait_send()
    step2 = squares_in(1, p1)
    resid_ref[...] = rhs - step1 * image1 - step2 * image2
    for j in range(own_cols):
        dens_ref[:, j * patch : (j + 1) * patch] = (
            step1 * g1_wide[j * d : (j + 1) * d] + step2 * g2_wide[j * d : (j + 1) * d]
        )
    sum_ref[...] = jnp.zeros((2 * d, patch), f32)

    @pl.when(odd == 0)
    def _():
        for s in range(2):
            remote(ev_out, ev_in.at[s], ev_ss, ev_rs.at[s], my_r, my_c).wait_recv()
        sum_ref[...] = ev_in[0].astype(f32) + ev_in[1].astype(f32)

    fc.wait_recv()
    field = sum_ref[...]
    for c in range(nc):
        field = field + fc_in[c].astype(f32)
    far = step1 * field[:d] + step2 * field[d:]
    for row in range(d):
        far_ref[:, row * patch : (row + 1) * patch] = far[row : row + 1]
    ev.wait_send()
    p1.wait_send()
    fc.wait_send()


def hand_on(*refs):
    count = len(refs) // 2
    for n in range(count):
        refs[count + n][...] = refs[n][...]


def per_device(nr, nc, right_side, u_factors, v_factors, ranks, far_blocks, block_target, recv_order):
    dens_count, patch = right_side.shape
    own_rows, all_cols, slot_count, _ = u_factors.shape
    group_rows, own_cols = v_factors.shape[:2]
    block_count, _, unknowns = far_blocks.shape
    recv_total = recv_order.shape[0]
    assert own_rows == 1 and group_rows == nc and all_cols == nc * own_cols
    assert block_count == 2 and recv_total == nr * nc and unknowns == own_cols * patch
    slots = own_cols * slot_count
    rows = own_cols * dens_count
    chunk = rows // nr
    half = -(-slots // (2 * LANES)) * LANES
    bf = jnp.bfloat16
    f32 = jnp.float32
    wire = bf if chunk % 16 == 0 else f32
    dma = pltpu.SemaphoreType.DMA
    pair = 2 if nc % 2 == 0 else 1
    u = u_factors.reshape(nc * slots, patch)
    v = v_factors.reshape(nc * slots, patch)
    vmem = pl.BlockSpec(memory_space=pltpu.VMEM)
    smem = pl.BlockSpec(memory_space=pltpu.SMEM)
    hbm = pl.BlockSpec(memory_space=pl.ANY)
    scratch = [
        pltpu.VMEM(u.shape, bf),
        pltpu.VMEM(v.shape, bf),
        pltpu.VMEM(far_blocks.shape, bf),
        pltpu.VMEM((2 * dens_count, unknowns), bf),
        pltpu.VMEM((nc // pair, pair * slots), f32),
        pltpu.VMEM((nr, chunk, patch), f32),
        pltpu.VMEM((2 * dens_count, patch), f32),
        pltpu.VMEM((4, nc, 2 * dens_count, half), bf),
        pltpu.VMEM((4, nc, 2 * dens_count, half), bf),
        pltpu.VMEM((2, nr, chunk, patch), wire),
        pltpu.VMEM((2, nr, chunk, patch), wire),
        pltpu.VMEM((2, nr, chunk, patch), wire),
        pltpu.VMEM((2, nc, dens_count, LANES), f32),
        pltpu.VMEM((2, nr, dens_count, LANES), f32),
        pltpu.VMEM((nr, 2 * dens_count, patch), bf),
        pltpu.VMEM((nc, 2 * dens_count, patch), bf),
        pltpu.VMEM((nc, 2 * dens_count, patch), bf),
        pltpu.VMEM((2 * dens_count, patch), bf),
        pltpu.VMEM((2, 2 * dens_count, patch), bf),
        dma((4,)),
        dma((4,)), dma((4,)),
        dma((2,)), dma((2,)),
        dma((2,)), dma((2,)),
        dma((2,)), dma((2,)),
        dma((2,)), dma((2,)),
        dma, dma,
        dma, dma,
        dma, dma((2,)),
    ]
    matrix = u.size + v.size
    results = pl.pallas_call(
        functools.partial(kernel, nr, nc, dens_count, own_cols, slot_count, patch, pair),
        out_shape=(
            jax.ShapeDtypeStruct((dens_count, unknowns), f32),
            jax.ShapeDtypeStruct((dens_count, patch), f32),
            jax.ShapeDtypeStruct((1, dens_count * patch), f32),
        ),
        in_specs=[vmem, vmem, smem, smem, hbm, hbm, hbm],
        out_specs=(vmem, vmem, vmem),
        scratch_shapes=scratch,
        compiler_params=pltpu.CompilerParams(
            collective_id=0, has_side_effects=True, vmem_limit_bytes=56 * 1024 * 1024
        ),
        cost_estimate=pl.CostEstimate(
            flops=8 * dens_count * matrix + 2 * dens_count * far_blocks.size,
            bytes_accessed=2 * (matrix + far_blocks.size), transcendentals=0,
        ),
    )(right_side, ranks, block_target, recv_order, u, v, far_blocks)
    return pl.pallas_call(
        hand_on,
        out_shape=tuple(jax.ShapeDtypeStruct(x.shape, x.dtype) for x in results),
        in_specs=[vmem] * len(results),
        out_specs=(vmem,) * len(results),
    )(*results)


def solution(mesh):
    return jax.shard_map(
        functools.partial(per_device, mesh.shape["row"], mesh.shape["col"]),
        mesh=mesh,
        in_specs=(
            P(None, ("row", "col")),
            P(("row", "col"), None, None, None),
            P("row", "col", None, None),
            P("row", "col"),
            P("row", None, "col"),
            P(),
            P(),
        ),
        out_specs=(P(None, "col"), P(None, ("row", "col")), P(("row", "col"), None)),
        check_vma=False,
    )
```

```python
import functools

import jax
import jax.numpy as jnp
from jax import lax
from jax.experimental import pallas as pl
from jax.experimental.pallas import tpu as pltpu
from jax.sharding import PartitionSpec as P

MESH = pl.DeviceIdType.MESH
LANES = 128
NT = (((1,), (1,)), ((), ()))
NN = (((1,), (0,)), ((), ()))


def partner_of(me, k, n):
    if n & (n - 1):
        return (me + k) % n
    out = 0
    bit = 1
    while bit < n:
        mine = (me // bit) % 2
        out = out + bit * ((1 - mine) if k & bit else mine)
        bit *= 2
    return out


def kernel(
    nr, nc, dens_count, own_cols, slot_count, patch, pair,
    rhs_hbm, ranks_hbm, target_hbm, order_hbm, u_hbm, v_hbm, f_hbm,
    dens_ref, resid_ref, far_ref,
    rhs_ref, ranks_ref, target_ref, order_ref,
    u_v, v_v, f_v, x_v, kept_ref, acc_ref, sum_ref,
    a2a_out, a2a_in, rs_out, rs_in, ag_buf, sc_col, sc_row, z_buf, fc_out, fc_in, ev_out, ev_in,
    small_sem, u_sem, v_sem, f_sem, a2a_ss, a2a_rs, rs_ss, rs_rs, ag_ss, ag_rs,
    scc_ss, scc_rs, scr_ss, scr_rs, z_ss, z_rs, fc_ss, fc_rs, ev_ss, ev_rs,
):
    d = dens_count
    slots = own_cols * slot_count
    half = a2a_out.shape[-1]
    rows = own_cols * d
    chunk = rows // nr
    groups = nc // pair
    wide = pair * slots
    part = patch // 2
    my_r = lax.axis_index("row")
    my_c = lax.axis_index("col")
    col_peers = [partner_of(my_c, k, nc) for k in range(nc - 1, 0, -1)]
    row_peers = [partner_of(my_r, k, nr) for k in range(nr - 1, 0, -1)]
    bf = jnp.bfloat16
    f32 = jnp.float32

    small = [
        pltpu.make_async_copy(src, dst, small_sem.at[n])
        for n, (src, dst) in enumerate(
            (
                (rhs_hbm, rhs_ref), (ranks_hbm, ranks_ref), (target_hbm, target_ref),
                (order_hbm, order_ref),
            )
        )
    ]
    u_copies, v_copies = [], []
    for q in range(groups):
        at = slice(q * wide, (q + 1) * wide)
        u_copies.append(pltpu.make_async_copy(u_hbm.at[at], u_v.at[at], u_sem.at[q]))
        v_copies.append(pltpu.make_async_copy(v_hbm.at[at], v_v.at[at], v_sem.at[q]))
    f_copies = []
    for b in range(2):
        for h in range(2):
            at = slice(h * part, (h + 1) * part)
            f_copies.append(
                pltpu.make_async_copy(f_hbm.at[b, at], f_v.at[b, at], f_sem.at[2 * b + h])
            )
    for copy in small[:2] + u_copies + small[2:]:
        copy.start()

    barrier = pltpu.get_barrier_semaphore()
    for to in col_peers:
        pl.semaphore_signal(barrier, inc=1, device_id=(my_r, to), device_id_type=MESH)
    for to in row_peers:
        pl.semaphore_signal(barrier, inc=1, device_id=(to, my_c), device_id_type=MESH)

    def remote(src, dst, ssem, rsem, r, c):
        return pltpu.make_async_remote_copy(
            src_ref=src, dst_ref=dst, send_sem=ssem, recv_sem=rsem,
            device_id=(r, c), device_id_type=MESH,
        )

    def over_col(out, into, ssem, rsem, shared=False):
        for to in col_peers:
            src = out.at[my_c] if shared else out.at[to]
            remote(src, into.at[my_c], ssem, rsem, my_r, to).start()
        return remote(out.at[: nc - 1], into.at[: nc - 1], ssem, rsem, my_r, my_c)

    def over_row(out, into, ssem, rsem, shared=False):
        for to in row_peers:
            src = out.at[my_r] if shared else out.at[to]
            remote(src, into.at[my_r], ssem, rsem, to, my_c).start()
        return remote(out.at[: nr - 1], into.at[: nr - 1], ssem, rsem, my_r, my_c)

    def pack(x):
        top, low = x[:, :half], x[:, half:]
        if low.shape[1] < half:
            low = jnp.concatenate([low, jnp.zeros((d, half - low.shape[1]), f32)], axis=1)
        return jnp.concatenate([top, low], axis=0).astype(bf)

    def unpack(x):
        x = x.astype(f32)
        return jnp.concatenate([x[:d], x[d:, : slots - half]], axis=1)

    lane_col = lax.broadcasted_iota(jnp.int32, (d, wide), 1) % slots // slot_count
    diag = jnp.concatenate([(lane_col == j).astype(f32) for j in range(own_cols)], axis=0)

    def put(rnd, q, value):
        for n in range(pair):
            a2a_out[rnd, q * pair + n] = pack(value[:, n * slots : (n + 1) * slots])

    def got(rnd, q):
        return jnp.concatenate([unpack(a2a_in[rnd, q * pair + n]) for n in range(pair)], axis=1)

    def exchange(rnd):
        sent = over_col(a2a_out.at[rnd], a2a_in.at[rnd], a2a_ss.at[rnd], a2a_rs.at[rnd])
        a2a_in[rnd, my_c] = a2a_out[rnd, my_c]
        return sent

    def back_of(rnd, r, first):
        rb = r.astype(bf)
        for q in range(groups):
            if first:
                u_copies[q].wait()
                v_copies[q].start()
            u = u_v[q * wide : (q + 1) * wide, :]
            put(rnd, q, lax.dot_general(rb, u, NT, preferred_element_type=f32))

    def image_of(rnd):
        image = jnp.zeros((d, patch), f32)
        for q in range(groups):
            u = u_v[q * wide : (q + 1) * wide, :]
            image = image + lax.dot_general(
                got(rnd, q).astype(bf), u, NN, preferred_element_type=f32
            )
        return image

    def grad_start(it, rnd):
        spread = []
        for q in range(groups):
            b = got(rnd, q) * kept_ref[q : q + 1, :]
            spread.append((jnp.concatenate([b] * own_cols, axis=0) * diag).astype(bf))
        sent = []
        for h in range(2):
            acc = jnp.zeros((rows, part), f32)
            for q in range(groups):
                v = v_v[q * wide : (q + 1) * wide, h * part : (h + 1) * part]
                acc = acc + lax.dot_general(spread[q], v, NN, preferred_element_type=f32)
            acc = acc.reshape(nr, chunk, part)
            rs_out[it, h] = acc.astype(rs_out.dtype)
            sent.append(
                over_row(rs_out.at[it, h], rs_in.at[it, h], rs_ss.at[it, h], rs_rs.at[it, h])
            )
            acc_ref[h] = acc
            rs_in[it, h, my_r] = jnp.zeros((chunk, part), rs_in.dtype)
        return sent

    def grad_end(it, h, sent):
        total = acc_ref[h, my_r]
        sent[h].wait_recv()
        for r in range(nr):
            total = total + rs_in[it, h, r].astype(f32)
        return total

    def gather_start(it, h, g):
        ag_buf[it, h, my_r] = g.astype(ag_buf.dtype)
        return over_row(
            ag_buf.at[it, h], ag_buf.at[it, h], ag_ss.at[it, h], ag_rs.at[it, h], shared=True
        )

    def gathered(it, h):
        return ag_buf[it, h].reshape(rows, part)

    def coef_of(rnd, it, sent):
        parts = [jnp.zeros((d, wide), f32)] * groups
        for h in range(2):
            sent[h].wait_recv()
            g = gathered(it, h).astype(bf)
            for q in range(groups):
                v = v_v[q * wide : (q + 1) * wide, h * part : (h + 1) * part]
                full = lax.dot_general(g, v, NT, preferred_element_type=f32) * diag
                for j in range(own_cols):
                    parts[q] = parts[q] + full[j * d : (j + 1) * d]
        for q in range(groups):
            put(rnd, q, parts[q] * kept_ref[q : q + 1, :])

    lane = lax.broadcasted_iota(jnp.int32, (d, LANES), 1)

    def squares_out(it, halves, image):
        squares = jnp.zeros((d, part), f32)
        for g in halves:
            for j in range(chunk // d):
                squares = squares + g[j * d : (j + 1) * d] * g[j * d : (j + 1) * d]
        grad_sq = jnp.sum(squares, axis=1, keepdims=True)
        image_sq = jnp.sum(image * image, axis=1, keepdims=True)
        sc_col[it, my_c] = jnp.where(lane < LANES // 2, grad_sq, image_sq)
        return over_col(
            sc_col.at[it], sc_col.at[it], scc_ss.at[it], scc_rs.at[it], shared=True
        )

    def squares_on(it, sent):
        sent.wait_recv()
        total = sc_col[it, 0]
        for c in range(1, nc):
            total = total + sc_col[it, c]
        sc_row[it, my_r] = total
        return over_row(
            sc_row.at[it], sc_row.at[it], scr_ss.at[it], scr_rs.at[it], shared=True
        )

    def squares_in(it, sent):
        sent.wait_recv()
        total = sc_row[it, 0]
        for r in range(1, nr):
            total = total + sc_row[it, r]
        return total[:, :1] / (total[:, LANES // 2 : LANES // 2 + 1] + 1e-6)

    small[1].wait()
    lane_all = lax.broadcasted_iota(jnp.int32, (nc, slots), 1)
    ranks = ranks_ref[...]
    limit = jnp.zeros((nc, slots), jnp.int32)
    for j in range(own_cols):
        limit = jnp.where(lane_all // slot_count == j, ranks[:, j : j + 1], limit)
    kept = (lane_all % slot_count < limit).astype(f32)
    for c in range(nc):
        at = pl.ds(c % pair * slots, slots)
        kept_ref[c // pair : c // pair + 1, at] = kept[c : c + 1]
    small[0].wait()
    rhs = rhs_ref[...]
    back_of(0, rhs, True)
    pl.semaphore_wait(barrier, nc - 1 + nr - 1)
    x0 = exchange(0)
    for copy in v_copies:
        copy.wait()
    for copy in f_copies[2:] + f_copies[:2]:
        copy.start()
    x0.wait_recv()
    s0 = grad_start(0, 0)
    x0.wait_send()
    g1, a0 = [], []
    for h in range(2):
        g1.append(grad_end(0, h, s0))
        a0.append(gather_start(0, h, g1[h]))
    for sent in s0:
        sent.wait_send()
    coef_of(1, 0, a0)
    x1 = exchange(1)
    for sent in a0:
        sent.wait_send()
    x1.wait_recv()
    image1 = image_of(1)
    back_of(2, image1, False)
    x2 = exchange(2)
    q0 = squares_out(0, g1, image1)
    x1.wait_send()
    x2.wait_recv()
    s1 = grad_start(1, 2)
    p0 = squares_on(0, q0)

    step1 = squares_in(0, p0)
    step_rows = jnp.concatenate([step1] * (chunk // d), axis=0)
    g2, a1 = [], []
    for h in range(2):
        g2.append(g1[h] - step_rows * grad_end(1, h, s1))
        a1.append(gather_start(1, h, g2[h]))
    x2.wait_send()
    for sent in s1:
        sent.wait_send()
    q0.wait_send()
    p0.wait_send()
    coef_of(3, 1, a1)
    x3 = exchange(3)

    for h in range(2):
        one, two = gathered(0, h).astype(f32), gathered(1, h).astype(f32)
        for j in range(own_cols):
            x_v[:, j * patch + h * part : j * patch + (h + 1) * part] = jnp.concatenate(
                [one[j * d : (j + 1) * d], two[j * d : (j + 1) * d]], axis=0
            ).astype(bf)

    def field_of(b):
        field = jnp.zeros((2 * d, patch), f32)
        for j in range(own_cols):
            at = slice(j * patch, (j + 1) * patch)
            field = field + lax.dot_general(
                x_v[:, at], f_v[b, :, at], NT, preferred_element_type=f32
            )
        return field.astype(bf)

    for copy in f_copies + small[2:]:
        copy.wait()
    z_buf[my_r] = field_of(1)
    z = over_row(z_buf, z_buf, z_ss, z_rs, shared=True)
    x3.wait_recv()
    image2 = image_of(3)
    q1 = squares_out(1, g2, image2)

    z.wait_recv()
    fields = [z_buf[r].astype(f32) for r in range(nr)]
    targets = [target_ref[2 * r + 1, my_c] for r in range(nr)]
    for to in range(nc):
        wanted = order_ref[my_r * nc + to]
        mixed = jnp.zeros((2 * d, patch), f32)
        for r in range(nr):
            mixed = mixed + fields[r] * jnp.where(targets[r] == wanted, 1.0, 0.0).astype(f32)
        fc_out[to] = mixed.astype(bf)
    fc = over_col(fc_out, fc_in, fc_ss, fc_rs)
    fc_in[my_c] = fc_out[my_c]

    ev_out[...] = field_of(0)
    odd = my_c % 2
    ev_row = (1 - odd) * ((my_r + nr // 2) % nr) + odd * my_r
    ev = remote(ev_out, ev_in.at[odd], ev_ss, ev_rs.at[odd], ev_row, my_c - odd)
    ev.start()
    p1 = squares_on(1, q1)
    x3.wait_send()
    for sent in a1:
        sent.wait_send()
    z.wait_send()
    q1.wait_send()
    fc.wait_recv()
    field = fc_in[0].astype(f32)
    for c in range(1, nc):
        field = field + fc_in[c].astype(f32)
    sum_ref[...] = field
    step2 = squares_in(1, p1)
    resid_ref[...] = rhs - step1 * image1 - step2 * image2
    for h in range(2):
        one, two = gathered(0, h).astype(f32), gathered(1, h).astype(f32)
        for j in range(own_cols):
            dens_ref[:, j * patch + h * part : j * patch + (h + 1) * part] = (
                step1 * one[j * d : (j + 1) * d] + step2 * two[j * d : (j + 1) * d]
            )

    @pl.when(odd == 0)
    def _():
        for s in range(2):
            remote(ev_out, ev_in.at[s], ev_ss, ev_rs.at[s], my_r, my_c).wait_recv()
        sum_ref[...] += ev_in[0].astype(f32) + ev_in[1].astype(f32)

    field = sum_ref[...]
    far = step1 * field[:d] + step2 * field[d:]
    for row in range(d):
        far_ref[:, row * patch : (row + 1) * patch] = far[row : row + 1]
    ev.wait_send()
    p1.wait_send()
    fc.wait_send()


def hand_on(*refs):
    count = len(refs) // 2
    for n in range(count):
        refs[count + n][...] = refs[n][...]


def per_device(nr, nc, right_side, u_factors, v_factors, ranks, far_blocks, block_target, recv_order):
    dens_count, patch = right_side.shape
    own_rows, all_cols, slot_count, _ = u_factors.shape
    group_rows, own_cols = v_factors.shape[:2]
    block_count, _, unknowns = far_blocks.shape
    recv_total = recv_order.shape[0]
    assert own_rows == 1 and group_rows == nc and all_cols == nc * own_cols
    assert block_count == 2 and recv_total == nr * nc and unknowns == own_cols * patch
    slots = own_cols * slot_count
    rows = own_cols * dens_count
    chunk = rows // nr
    part = patch // 2
    half = -(-slots // (2 * LANES)) * LANES
    bf = jnp.bfloat16
    f32 = jnp.float32
    wire = bf if chunk % 16 == 0 else f32
    dma = pltpu.SemaphoreType.DMA
    pair = 2 if nc % 2 == 0 else 1
    u = u_factors.reshape(nc * slots, patch)
    v = v_factors.reshape(nc * slots, patch)
    vmem = pl.BlockSpec(memory_space=pltpu.VMEM)
    hbm = pl.BlockSpec(memory_space=pl.ANY)
    scratch = [
        pltpu.VMEM(right_side.shape, f32),
        pltpu.VMEM(ranks.shape, jnp.int32),
        pltpu.SMEM(block_target.shape, jnp.int32),
        pltpu.SMEM(recv_order.shape, jnp.int32),
        pltpu.VMEM(u.shape, bf),
        pltpu.VMEM(v.shape, bf),
        pltpu.VMEM(far_blocks.shape, bf),
        pltpu.VMEM((2 * dens_count, unknowns), bf),
        pltpu.VMEM((nc // pair, pair * slots), f32),
        pltpu.VMEM((2, nr, chunk, part), f32),
        pltpu.VMEM((2 * dens_count, patch), f32),
        pltpu.VMEM((4, nc, 2 * dens_count, half), bf),
        pltpu.VMEM((4, nc, 2 * dens_count, half), bf),
        pltpu.VMEM((2, 2, nr, chunk, part), wire),
        pltpu.VMEM((2, 2, nr, chunk, part), wire),
        pltpu.VMEM((2, 2, nr, chunk, part), wire),
        pltpu.VMEM((2, nc, dens_count, LANES), f32),
        pltpu.VMEM((2, nr, dens_count, LANES), f32),
        pltpu.VMEM((nr, 2 * dens_count, patch), bf),
        pltpu.VMEM((nc, 2 * dens_count, patch), bf),
        pltpu.VMEM((nc, 2 * dens_count, patch), bf),
        pltpu.VMEM((2 * dens_count, patch), bf),
        pltpu.VMEM((2, 2 * dens_count, patch), bf),
        dma((4,)), dma((nc // pair,)), dma((nc // pair,)), dma((4,)),
        dma((4,)), dma((4,)),
        dma((2, 2)), dma((2, 2)),
        dma((2, 2)), dma((2, 2)),
        dma((2,)), dma((2,)),
        dma((2,)), dma((2,)),
        dma, dma,
        dma, dma,
        dma, dma((2,)),
    ]
    matrix = u.size + v.size
    results = pl.pallas_call(
        functools.partial(kernel, nr, nc, dens_count, own_cols, slot_count, patch, pair),
        out_shape=(
            jax.ShapeDtypeStruct((dens_count, unknowns), f32),
            jax.ShapeDtypeStruct((dens_count, patch), f32),
            jax.ShapeDtypeStruct((1, dens_count * patch), f32),
        ),
        in_specs=[hbm] * 7,
        out_specs=(vmem, vmem, vmem),
        scratch_shapes=scratch,
        compiler_params=pltpu.CompilerParams(
            collective_id=0, has_side_effects=True, vmem_limit_bytes=56 * 1024 * 1024
        ),
        cost_estimate=pl.CostEstimate(
            flops=8 * dens_count * matrix + 2 * dens_count * far_blocks.size,
            bytes_accessed=2 * (matrix + far_blocks.size), transcendentals=0,
        ),
    )(right_side, ranks, block_target, recv_order, u, v, far_blocks)
    return pl.pallas_call(
        hand_on,
        out_shape=tuple(jax.ShapeDtypeStruct(x.shape, x.dtype) for x in results),
        in_specs=[vmem] * len(results),
        out_specs=(vmem,) * len(results),
    )(*results)


def solution(mesh):
    return jax.shard_map(
        functools.partial(per_device, mesh.shape["row"], mesh.shape["col"]),
        mesh=mesh,
        in_specs=(
            P(None, ("row", "col")),
            P(("row", "col"), None, None, None),
            P("row", "col", None, None),
            P("row", "col"),
            P("row", None, "col"),
            P(),
            P(),
        ),
        out_specs=(P(None, "col"), P(None, ("row", "col")), P(("row", "col"), None)),
        check_vma=False,
    )
```

```python
import functools

import jax
import jax.numpy as jnp
from jax import lax
from jax.experimental import pallas as pl
from jax.experimental.pallas import tpu as pltpu
from jax.sharding import PartitionSpec as P

MESH = pl.DeviceIdType.MESH
LANES = 128
NT = (((1,), (1,)), ((), ()))
NN = (((1,), (0,)), ((), ()))


def partner_of(me, k, n):
    if n & (n - 1):
        return (me + k) % n
    out = 0
    bit = 1
    while bit < n:
        mine = (me // bit) % 2
        out = out + bit * ((1 - mine) if k & bit else mine)
        bit *= 2
    return out


def kernel(
    nr, nc, dens_count, own_cols, slot_count, patch, pair,
    rhs_hbm, ranks_hbm, target_hbm, order_hbm, u_hbm, v_hbm, f_hbm,
    dens_ref, resid_ref, far_ref,
    rhs_ref, ranks_ref, target_ref, order_ref,
    u_v, v_v, f_v, x_v, kept_ref, g_ref, sum_ref,
    a2a_out, a2a_in, rd_out, rd_in, sc_col, sc_row, z_buf, fc_out, fc_in, ev_out, ev_in,
    small_sem, u_sem, v_sem, f_sem, a2a_ss, a2a_rs, rd_ss, rd_rs,
    scc_ss, scc_rs, scr_ss, scr_rs, z_ss, z_rs, fc_ss, fc_rs, ev_ss, ev_rs,
):
    d = dens_count
    slots = own_cols * slot_count
    half = a2a_out.shape[-1]
    rows = own_cols * d
    groups = nc // pair
    stages = rd_out.shape[2]
    wide = pair * slots
    part = patch // 2
    my_r = lax.axis_index("row")
    my_c = lax.axis_index("col")
    col_peers = [partner_of(my_c, k, nc) for k in range(nc - 1, 0, -1)]
    row_peers = [partner_of(my_r, k, nr) for k in range(nr - 1, 0, -1)]
    bf = jnp.bfloat16
    f32 = jnp.float32

    small = [
        pltpu.make_async_copy(src, dst, small_sem.at[n])
        for n, (src, dst) in enumerate(
            (
                (rhs_hbm, rhs_ref), (ranks_hbm, ranks_ref), (target_hbm, target_ref),
                (order_hbm, order_ref),
            )
        )
    ]
    u_copies, v_copies = [], []
    for q in range(groups):
        at = slice(q * wide, (q + 1) * wide)
        u_copies.append(pltpu.make_async_copy(u_hbm.at[at], u_v.at[at], u_sem.at[q]))
        v_copies.append(pltpu.make_async_copy(v_hbm.at[at], v_v.at[at], v_sem.at[q]))
    f_copies = []
    for b in range(2):
        for h in range(2):
            at = slice(h * part, (h + 1) * part)
            f_copies.append(
                pltpu.make_async_copy(f_hbm.at[b, at], f_v.at[b, at], f_sem.at[2 * b + h])
            )
    for copy in small[:2] + u_copies + small[2:]:
        copy.start()

    barrier = pltpu.get_barrier_semaphore()
    for to in col_peers:
        pl.semaphore_signal(barrier, inc=1, device_id=(my_r, to), device_id_type=MESH)
    for to in row_peers:
        pl.semaphore_signal(barrier, inc=1, device_id=(to, my_c), device_id_type=MESH)

    def remote(src, dst, ssem, rsem, r, c):
        return pltpu.make_async_remote_copy(
            src_ref=src, dst_ref=dst, send_sem=ssem, recv_sem=rsem,
            device_id=(r, c), device_id_type=MESH,
        )

    def over_col(out, into, ssem, rsem, shared=False):
        for to in col_peers:
            src = out.at[my_c] if shared else out.at[to]
            remote(src, into.at[my_c], ssem, rsem, my_r, to).start()
        return remote(out.at[: nc - 1], into.at[: nc - 1], ssem, rsem, my_r, my_c)

    def over_row(out, into, ssem, rsem, shared=False):
        for to in row_peers:
            src = out.at[my_r] if shared else out.at[to]
            remote(src, into.at[my_r], ssem, rsem, to, my_c).start()
        return remote(out.at[: nr - 1], into.at[: nr - 1], ssem, rsem, my_r, my_c)

    def pack(x):
        top, low = x[:, :half], x[:, half:]
        if low.shape[1] < half:
            low = jnp.concatenate([low, jnp.zeros((d, half - low.shape[1]), f32)], axis=1)
        return jnp.concatenate([top, low], axis=0).astype(bf)

    def unpack(x):
        x = x.astype(f32)
        return jnp.concatenate([x[:d], x[d:, : slots - half]], axis=1)

    lane_col = lax.broadcasted_iota(jnp.int32, (d, wide), 1) % slots // slot_count
    diag = jnp.concatenate([(lane_col == j).astype(f32) for j in range(own_cols)], axis=0)

    def put(rnd, q, value):
        for n in range(pair):
            a2a_out[rnd, q * pair + n] = pack(value[:, n * slots : (n + 1) * slots])

    def got(rnd, q):
        return jnp.concatenate([unpack(a2a_in[rnd, q * pair + n]) for n in range(pair)], axis=1)

    def exchange(rnd):
        sent = over_col(a2a_out.at[rnd], a2a_in.at[rnd], a2a_ss.at[rnd], a2a_rs.at[rnd])
        a2a_in[rnd, my_c] = a2a_out[rnd, my_c]
        return sent

    def back_of(rnd, r, first):
        rb = r.astype(bf)
        for q in range(groups):
            if first:
                u_copies[q].wait()
                v_copies[q].start()
            u = u_v[q * wide : (q + 1) * wide, :]
            put(rnd, q, lax.dot_general(rb, u, NT, preferred_element_type=f32))

    def image_of(rnd):
        image = jnp.zeros((d, patch), f32)
        for q in range(groups):
            u = u_v[q * wide : (q + 1) * wide, :]
            image = image + lax.dot_general(
                got(rnd, q).astype(bf), u, NN, preferred_element_type=f32
            )
        return image

    def grad_start(it, rnd):
        spread = []
        for q in range(groups):
            b = got(rnd, q) * kept_ref[q : q + 1, :]
            spread.append((jnp.concatenate([b] * own_cols, axis=0) * diag).astype(bf))
        sent = []
        for h in range(2):
            acc = jnp.zeros((rows, part), f32)
            for q in range(groups):
                v = v_v[q * wide : (q + 1) * wide, h * part : (h + 1) * part]
                acc = acc + lax.dot_general(spread[q], v, NN, preferred_element_type=f32)
            sent.append(double(it, h, 0, acc))
        return sent

    def double(it, h, stage, value):
        rd_out[it, h, stage] = value.astype(bf)
        copy = remote(
            rd_out.at[it, h, stage], rd_in.at[it, h, stage], rd_ss.at[it, h, stage],
            rd_rs.at[it, h, stage], partner_of(my_r, 1 << stage, nr), my_c,
        )
        copy.start()
        return copy

    def doubled(it, h, stage, copy):
        copy.wait_recv()
        return rd_out[it, h, stage].astype(f32) + rd_in[it, h, stage].astype(f32)

    def grad_on(it, sent):
        flying, done = list(sent), list(sent)
        for stage in range(stages - 1):
            for h in range(2):
                value = doubled(it, h, stage, flying[h])
                flying[h] = double(it, h, stage + 1, value)
                done.append(flying[h])
        return flying, done

    def coef_of(rnd, it, flying, step):
        parts = [jnp.zeros((d, wide), f32)] * groups
        for h in range(2):
            g = doubled(it, h, stages - 1, flying[h])
            if step is not None:
                g = g_ref[0, h] - jnp.concatenate([step] * own_cols, axis=0) * g
            g_ref[it, h] = g
            g = g.astype(bf)
            for q in range(groups):
                v = v_v[q * wide : (q + 1) * wide, h * part : (h + 1) * part]
                full = lax.dot_general(g, v, NT, preferred_element_type=f32) * diag
                for j in range(own_cols):
                    parts[q] = parts[q] + full[j * d : (j + 1) * d]
        for q in range(groups):
            put(rnd, q, parts[q] * kept_ref[q : q + 1, :])

    lane = lax.broadcasted_iota(jnp.int32, (d, LANES), 1)

    def squares_out(it, image):
        squares = jnp.zeros((d, part), f32)
        for h in range(2):
            for j in range(own_cols):
                g = g_ref[it, h, j * d : (j + 1) * d]
                squares = squares + g * g
        grad_sq = jnp.sum(squares, axis=1, keepdims=True) * (1.0 / nr)
        image_sq = jnp.sum(image * image, axis=1, keepdims=True)
        sc_col[it, my_c] = jnp.where(lane < LANES // 2, grad_sq, image_sq)
        return over_col(
            sc_col.at[it], sc_col.at[it], scc_ss.at[it], scc_rs.at[it], shared=True
        )

    def squares_on(it, sent):
        sent.wait_recv()
        total = sc_col[it, 0]
        for c in range(1, nc):
            total = total + sc_col[it, c]
        sc_row[it, my_r] = total
        return over_row(
            sc_row.at[it], sc_row.at[it], scr_ss.at[it], scr_rs.at[it], shared=True
        )

    def squares_in(it, sent):
        sent.wait_recv()
        total = sc_row[it, 0]
        for r in range(1, nr):
            total = total + sc_row[it, r]
        return total[:, :1] / (total[:, LANES // 2 : LANES // 2 + 1] + 1e-6)

    small[1].wait()
    lane_all = lax.broadcasted_iota(jnp.int32, (nc, slots), 1)
    ranks = ranks_ref[...]
    limit = jnp.zeros((nc, slots), jnp.int32)
    for j in range(own_cols):
        limit = jnp.where(lane_all // slot_count == j, ranks[:, j : j + 1], limit)
    kept = (lane_all % slot_count < limit).astype(f32)
    for c in range(nc):
        at = pl.ds(c % pair * slots, slots)
        kept_ref[c // pair : c // pair + 1, at] = kept[c : c + 1]
    small[0].wait()
    rhs = rhs_ref[...]
    back_of(0, rhs, True)
    pl.semaphore_wait(barrier, nc - 1 + nr - 1)
    x0 = exchange(0)
    for copy in v_copies:
        copy.wait()
    for copy in f_copies[2:] + f_copies[:2]:
        copy.start()
    x0.wait_recv()
    s0 = grad_start(0, 0)
    x0.wait_send()
    flying, s0 = grad_on(0, s0)
    coef_of(1, 0, flying, None)
    x1 = exchange(1)
    for sent in s0:
        sent.wait_send()
    x1.wait_recv()
    image1 = image_of(1)
    back_of(2, image1, False)
    x2 = exchange(2)
    q0 = squares_out(0, image1)
    x1.wait_send()
    x2.wait_recv()
    s1 = grad_start(1, 2)
    p0 = squares_on(0, q0)

    flying, s1 = grad_on(1, s1)
    x2.wait_send()
    q0.wait_send()
    step1 = squares_in(0, p0)
    coef_of(3, 1, flying, step1)
    x3 = exchange(3)

    for h in range(2):
        one, two = g_ref[0, h], g_ref[1, h]
        for j in range(own_cols):
            x_v[:, j * patch + h * part : j * patch + (h + 1) * part] = jnp.concatenate(
                [one[j * d : (j + 1) * d], two[j * d : (j + 1) * d]], axis=0
            ).astype(bf)

    def field_of(b):
        field = jnp.zeros((2 * d, patch), f32)
        for j in range(own_cols):
            at = slice(j * patch, (j + 1) * patch)
            field = field + lax.dot_general(
                x_v[:, at], f_v[b, :, at], NT, preferred_element_type=f32
            )
        return field.astype(bf)

    for copy in f_copies + small[2:]:
        copy.wait()
    z_buf[my_r] = field_of(1)
    z = over_row(z_buf, z_buf, z_ss, z_rs, shared=True)
    x3.wait_recv()
    image2 = image_of(3)
    q1 = squares_out(1, image2)

    z.wait_recv()
    fields = [z_buf[r].astype(f32) for r in range(nr)]
    targets = [target_ref[2 * r + 1, my_c] for r in range(nr)]
    for to in range(nc):
        wanted = order_ref[my_r * nc + to]
        mixed = jnp.zeros((2 * d, patch), f32)
        for r in range(nr):
            mixed = mixed + fields[r] * jnp.where(targets[r] == wanted, 1.0, 0.0).astype(f32)
        fc_out[to] = mixed.astype(bf)
    fc = over_col(fc_out, fc_in, fc_ss, fc_rs)
    fc_in[my_c] = fc_out[my_c]

    ev_out[...] = field_of(0)
    odd = my_c % 2
    ev_row = (1 - odd) * ((my_r + nr // 2) % nr) + odd * my_r
    ev = remote(ev_out, ev_in.at[odd], ev_ss, ev_rs.at[odd], ev_row, my_c - odd)
    ev.start()
    p1 = squares_on(1, q1)
    x3.wait_send()
    p0.wait_send()
    for sent in s1:
        sent.wait_send()
    z.wait_send()
    q1.wait_send()
    fc.wait_recv()
    field = fc_in[0].astype(f32)
    for c in range(1, nc):
        field = field + fc_in[c].astype(f32)
    sum_ref[...] = field
    step2 = squares_in(1, p1)
    resid_ref[...] = rhs - step1 * image1 - step2 * image2
    for h in range(2):
        one, two = g_ref[0, h], g_ref[1, h]
        for j in range(own_cols):
            dens_ref[:, j * patch + h * part : j * patch + (h + 1) * part] = (
                step1 * one[j * d : (j + 1) * d] + step2 * two[j * d : (j + 1) * d]
            )

    @pl.when(odd == 0)
    def _():
        for s in range(2):
            remote(ev_out, ev_in.at[s], ev_ss, ev_rs.at[s], my_r, my_c).wait_recv()
        sum_ref[...] += ev_in[0].astype(f32) + ev_in[1].astype(f32)

    field = sum_ref[...]
    far = step1 * field[:d] + step2 * field[d:]
    for row in range(d):
        far_ref[:, row * patch : (row + 1) * patch] = far[row : row + 1]
    ev.wait_send()
    p1.wait_send()
    fc.wait_send()


def hand_on(*refs):
    count = len(refs) // 2
    for n in range(count):
        refs[count + n][...] = refs[n][...]


def per_device(nr, nc, right_side, u_factors, v_factors, ranks, far_blocks, block_target, recv_order):
    dens_count, patch = right_side.shape
    own_rows, all_cols, slot_count, _ = u_factors.shape
    group_rows, own_cols = v_factors.shape[:2]
    block_count, _, unknowns = far_blocks.shape
    recv_total = recv_order.shape[0]
    assert own_rows == 1 and group_rows == nc and all_cols == nc * own_cols
    assert block_count == 2 and recv_total == nr * nc and unknowns == own_cols * patch
    slots = own_cols * slot_count
    rows = own_cols * dens_count
    part = patch // 2
    stages = nr.bit_length() - 1
    assert nr == 1 << stages
    half = -(-slots // (2 * LANES)) * LANES
    bf = jnp.bfloat16
    f32 = jnp.float32
    dma = pltpu.SemaphoreType.DMA
    pair = 2 if nc % 2 == 0 else 1
    u = u_factors.reshape(nc * slots, patch)
    v = v_factors.reshape(nc * slots, patch)
    vmem = pl.BlockSpec(memory_space=pltpu.VMEM)
    hbm = pl.BlockSpec(memory_space=pl.ANY)
    scratch = [
        pltpu.VMEM(right_side.shape, f32),
        pltpu.VMEM(ranks.shape, jnp.int32),
        pltpu.SMEM(block_target.shape, jnp.int32),
        pltpu.SMEM(recv_order.shape, jnp.int32),
        pltpu.VMEM(u.shape, bf),
        pltpu.VMEM(v.shape, bf),
        pltpu.VMEM(far_blocks.shape, bf),
        pltpu.VMEM((2 * dens_count, unknowns), bf),
        pltpu.VMEM((nc // pair, pair * slots), f32),
        pltpu.VMEM((2, 2, rows, part), f32),
        pltpu.VMEM((2 * dens_count, patch), f32),
        pltpu.VMEM((4, nc, 2 * dens_count, half), bf),
        pltpu.VMEM((4, nc, 2 * dens_count, half), bf),
        pltpu.VMEM((2, 2, stages, rows, part), bf),
        pltpu.VMEM((2, 2, stages, rows, part), bf),
        pltpu.VMEM((2, nc, dens_count, LANES), f32),
        pltpu.VMEM((2, nr, dens_count, LANES), f32),
        pltpu.VMEM((nr, 2 * dens_count, patch), bf),
        pltpu.VMEM((nc, 2 * dens_count, patch), bf),
        pltpu.VMEM((nc, 2 * dens_count, patch), bf),
        pltpu.VMEM((2 * dens_count, patch), bf),
        pltpu.VMEM((2, 2 * dens_count, patch), bf),
        dma((4,)), dma((nc // pair,)), dma((nc // pair,)), dma((4,)),
        dma((4,)), dma((4,)),
        dma((2, 2, stages)), dma((2, 2, stages)),
        dma((2,)), dma((2,)),
        dma((2,)), dma((2,)),
        dma, dma,
        dma, dma,
        dma, dma((2,)),
    ]
    matrix = u.size + v.size
    results = pl.pallas_call(
        functools.partial(kernel, nr, nc, dens_count, own_cols, slot_count, patch, pair),
        out_shape=(
            jax.ShapeDtypeStruct((dens_count, unknowns), f32),
            jax.ShapeDtypeStruct((dens_count, patch), f32),
            jax.ShapeDtypeStruct((1, dens_count * patch), f32),
        ),
        in_specs=[hbm] * 7,
        out_specs=(vmem, vmem, vmem),
        scratch_shapes=scratch,
        compiler_params=pltpu.CompilerParams(
            collective_id=0, has_side_effects=True, vmem_limit_bytes=56 * 1024 * 1024
        ),
        cost_estimate=pl.CostEstimate(
            flops=8 * dens_count * matrix + 2 * dens_count * far_blocks.size,
            bytes_accessed=2 * (matrix + far_blocks.size), transcendentals=0,
        ),
    )(right_side, ranks, block_target, recv_order, u, v, far_blocks)
    return pl.pallas_call(
        hand_on,
        out_shape=tuple(jax.ShapeDtypeStruct(x.shape, x.dtype) for x in results),
        in_specs=[vmem] * len(results),
        out_specs=(vmem,) * len(results),
    )(*results)


def solution(mesh):
    return jax.shard_map(
        functools.partial(per_device, mesh.shape["row"], mesh.shape["col"]),
        mesh=mesh,
        in_specs=(
            P(None, ("row", "col")),
            P(("row", "col"), None, None, None),
            P("row", "col", None, None),
            P("row", "col"),
            P("row", None, "col"),
            P(),
            P(),
        ),
        out_specs=(P(None, "col"), P(None, ("row", "col")), P(("row", "col"), None)),
        check_vma=False,
    )
```

```python
import functools

import jax
import jax.numpy as jnp
from jax import lax
from jax.experimental import pallas as pl
from jax.experimental.pallas import tpu as pltpu
from jax.sharding import PartitionSpec as P

MESH = pl.DeviceIdType.MESH
LANES = 128
NT = (((1,), (1,)), ((), ()))
NN = (((1,), (0,)), ((), ()))


def partner_of(me, k, n):
    if n & (n - 1):
        return (me + k) % n
    out = 0
    bit = 1
    while bit < n:
        mine = (me // bit) % 2
        out = out + bit * ((1 - mine) if k & bit else mine)
        bit *= 2
    return out


def kernel(
    nr, nc, dens_count, own_cols, slot_count, patch, pair,
    rhs_hbm, ranks_hbm, target_hbm, order_hbm, u_hbm, v_hbm, f_hbm,
    dens_ref, resid_ref, far_ref,
    rhs_ref, ranks_ref, target_ref, order_ref,
    u_v, v_v, f_v, x_v, kept_ref, g_ref, sum_ref,
    a2a_out, a2a_in, rd_out, rd_in, sc_col, sc_row, z_buf, fc_out, fc_in, ev_out, ev_in,
    small_sem, u_sem, v_sem, f_sem, a2a_ss, a2a_rs, rd_ss, rd_rs,
    scc_ss, scc_rs, scr_ss, scr_rs, z_ss, z_rs, fc_ss, fc_rs, ev_ss, ev_rs,
):
    d = dens_count
    slots = own_cols * slot_count
    half = a2a_out.shape[-1]
    rows = own_cols * d
    groups = nc // pair
    stages = rd_out.shape[2]
    wide = pair * slots
    part = patch // 2
    my_r = lax.axis_index("row")
    my_c = lax.axis_index("col")
    col_peers = [partner_of(my_c, k, nc) for k in range(nc - 1, 0, -1)]
    row_peers = [partner_of(my_r, k, nr) for k in range(nr - 1, 0, -1)]
    bf = jnp.bfloat16
    f32 = jnp.float32

    small = [
        pltpu.make_async_copy(src, dst, small_sem.at[n])
        for n, (src, dst) in enumerate(
            (
                (rhs_hbm, rhs_ref), (ranks_hbm, ranks_ref), (target_hbm, target_ref),
                (order_hbm, order_ref),
            )
        )
    ]
    u_copies, v_copies = [], []
    order = [partner_of(my_c // pair, k, groups) for k in range(groups - 1, -1, -1)]
    for n in range(groups):
        at = pl.ds(pl.multiple_of(order[n] * wide, wide), wide)
        u_copies.append(pltpu.make_async_copy(u_hbm.at[at], u_v.at[at], u_sem.at[n]))
        v_copies.append(pltpu.make_async_copy(v_hbm.at[at], v_v.at[at], v_sem.at[n]))
    f_copies = []
    for b in range(2):
        for h in range(2):
            at = slice(h * part, (h + 1) * part)
            f_copies.append(
                pltpu.make_async_copy(f_hbm.at[b, at], f_v.at[b, at], f_sem.at[2 * b + h])
            )
    for copy in small[:2] + u_copies + small[2:]:
        copy.start()

    barrier = pltpu.get_barrier_semaphore()
    for to in col_peers:
        pl.semaphore_signal(barrier, inc=1, device_id=(my_r, to), device_id_type=MESH)
    for to in row_peers:
        pl.semaphore_signal(barrier, inc=1, device_id=(to, my_c), device_id_type=MESH)

    def remote(src, dst, ssem, rsem, r, c):
        return pltpu.make_async_remote_copy(
            src_ref=src, dst_ref=dst, send_sem=ssem, recv_sem=rsem,
            device_id=(r, c), device_id_type=MESH,
        )

    def over_col(out, into, ssem, rsem, shared=False):
        for to in col_peers:
            src = out.at[my_c] if shared else out.at[to]
            remote(src, into.at[my_c], ssem, rsem, my_r, to).start()
        return remote(out.at[: nc - 1], into.at[: nc - 1], ssem, rsem, my_r, my_c)

    def over_row(out, into, ssem, rsem, shared=False):
        for to in row_peers:
            src = out.at[my_r] if shared else out.at[to]
            remote(src, into.at[my_r], ssem, rsem, to, my_c).start()
        return remote(out.at[: nr - 1], into.at[: nr - 1], ssem, rsem, my_r, my_c)

    def pack(x):
        top, low = x[:, :half], x[:, half:]
        if low.shape[1] < half:
            low = jnp.concatenate([low, jnp.zeros((d, half - low.shape[1]), f32)], axis=1)
        return jnp.concatenate([top, low], axis=0).astype(bf)

    def unpack(x):
        x = x.astype(f32)
        return jnp.concatenate([x[:d], x[d:, : slots - half]], axis=1)

    lane_col = lax.broadcasted_iota(jnp.int32, (d, wide), 1) % slots // slot_count
    diag = jnp.concatenate([(lane_col == j).astype(f32) for j in range(own_cols)], axis=0)

    def put(rnd, q, value):
        for n in range(pair):
            a2a_out[rnd, q * pair + n] = pack(value[:, n * slots : (n + 1) * slots])

    def got(rnd, q):
        return jnp.concatenate([unpack(a2a_in[rnd, q * pair + n]) for n in range(pair)], axis=1)

    def post(rnd, n):
        if n < groups - 1:
            peers = [order[n] * pair + m for m in range(pair)]
        else:
            peers = [my_c // pair * pair + (my_c + m) % pair for m in range(1, pair)]
        for to in peers:
            remote(
                a2a_out.at[rnd, to], a2a_in.at[rnd, my_c], a2a_ss.at[rnd], a2a_rs.at[rnd], my_r, to
            ).start()

    def posted(rnd):
        a2a_in[rnd, my_c] = a2a_out[rnd, my_c]
        return remote(
            a2a_out.at[rnd, : nc - 1], a2a_in.at[rnd, : nc - 1], a2a_ss.at[rnd],
            a2a_rs.at[rnd], my_r, my_c,
        )

    def back_of(rnd, r, first):
        rb = r.astype(bf)
        for n in range(groups):
            if first:
                u_copies[n].wait()
                v_copies[n].start()
            u = u_v[pl.ds(pl.multiple_of(order[n] * wide, wide), wide), :]
            put(rnd, order[n], lax.dot_general(rb, u, NT, preferred_element_type=f32))
            if first and n == 0:
                pl.semaphore_wait(barrier, nc - 1 + nr - 1)
            post(rnd, n)
        return posted(rnd)

    def image_of(rnd):
        image = jnp.zeros((d, patch), f32)
        for q in range(groups):
            u = u_v[q * wide : (q + 1) * wide, :]
            image = image + lax.dot_general(
                got(rnd, q).astype(bf), u, NN, preferred_element_type=f32
            )
        return image

    def grad_start(it, rnd):
        spread = []
        for q in range(groups):
            b = got(rnd, q) * kept_ref[q : q + 1, :]
            spread.append((jnp.concatenate([b] * own_cols, axis=0) * diag).astype(bf))
        sent = []
        for h in range(2):
            acc = jnp.zeros((rows, part), f32)
            for q in range(groups):
                v = v_v[q * wide : (q + 1) * wide, h * part : (h + 1) * part]
                acc = acc + lax.dot_general(spread[q], v, NN, preferred_element_type=f32)
            sent.append(double(it, h, 0, acc))
        return sent

    def double(it, h, stage, value):
        rd_out[it, h, stage] = value.astype(bf)
        copy = remote(
            rd_out.at[it, h, stage], rd_in.at[it, h, stage], rd_ss.at[it, h, stage],
            rd_rs.at[it, h, stage], partner_of(my_r, 1 << stage, nr), my_c,
        )
        copy.start()
        return copy

    def doubled(it, h, stage, copy):
        copy.wait_recv()
        return rd_out[it, h, stage].astype(f32) + rd_in[it, h, stage].astype(f32)

    def grad_on(it, sent):
        flying, done = list(sent), list(sent)
        for stage in range(stages - 1):
            for h in range(2):
                value = doubled(it, h, stage, flying[h])
                flying[h] = double(it, h, stage + 1, value)
                done.append(flying[h])
        return flying, done

    def coef_of(rnd, it, flying, step):
        parts = [jnp.zeros((d, wide), f32)] * groups
        for h in range(2):
            g = doubled(it, h, stages - 1, flying[h])
            if step is not None:
                g = g_ref[0, h] - jnp.concatenate([step] * own_cols, axis=0) * g
            g_ref[it, h] = g
            g = g.astype(bf)
            for n in range(groups):
                at = pl.ds(pl.multiple_of(order[n] * wide, wide), wide)
                v = v_v[at, h * part : (h + 1) * part]
                full = lax.dot_general(g, v, NT, preferred_element_type=f32) * diag
                for j in range(own_cols):
                    parts[n] = parts[n] + full[j * d : (j + 1) * d]
                if h == 1:
                    put(rnd, order[n], parts[n] * kept_ref[pl.ds(order[n], 1), :])
                    post(rnd, n)
        return posted(rnd)

    lane = lax.broadcasted_iota(jnp.int32, (d, LANES), 1)

    def squares_out(it, image):
        squares = jnp.zeros((d, part), f32)
        for h in range(2):
            for j in range(own_cols):
                g = g_ref[it, h, j * d : (j + 1) * d]
                squares = squares + g * g
        grad_sq = jnp.sum(squares, axis=1, keepdims=True) * (1.0 / nr)
        image_sq = jnp.sum(image * image, axis=1, keepdims=True)
        sc_col[it, my_c] = jnp.where(lane < LANES // 2, grad_sq, image_sq)
        return over_col(
            sc_col.at[it], sc_col.at[it], scc_ss.at[it], scc_rs.at[it], shared=True
        )

    def squares_on(it, sent):
        sent.wait_recv()
        total = sc_col[it, 0]
        for c in range(1, nc):
            total = total + sc_col[it, c]
        sc_row[it, my_r] = total
        return over_row(
            sc_row.at[it], sc_row.at[it], scr_ss.at[it], scr_rs.at[it], shared=True
        )

    def squares_in(it, sent):
        sent.wait_recv()
        total = sc_row[it, 0]
        for r in range(1, nr):
            total = total + sc_row[it, r]
        return total[:, :1] / (total[:, LANES // 2 : LANES // 2 + 1] + 1e-6)

    small[1].wait()
    lane_all = lax.broadcasted_iota(jnp.int32, (nc, slots), 1)
    ranks = ranks_ref[...]
    limit = jnp.zeros((nc, slots), jnp.int32)
    for j in range(own_cols):
        limit = jnp.where(lane_all // slot_count == j, ranks[:, j : j + 1], limit)
    kept = (lane_all % slot_count < limit).astype(f32)
    for c in range(nc):
        at = pl.ds(c % pair * slots, slots)
        kept_ref[c // pair : c // pair + 1, at] = kept[c : c + 1]
    small[0].wait()
    rhs = rhs_ref[...]
    x0 = back_of(0, rhs, True)
    for copy in v_copies:
        copy.wait()
    for copy in f_copies[2:] + f_copies[:2]:
        copy.start()
    x0.wait_recv()
    s0 = grad_start(0, 0)
    x0.wait_send()
    flying, s0 = grad_on(0, s0)
    x1 = coef_of(1, 0, flying, None)
    for sent in s0:
        sent.wait_send()
    x1.wait_recv()
    image1 = image_of(1)
    x2 = back_of(2, image1, False)
    q0 = squares_out(0, image1)
    x1.wait_send()
    x2.wait_recv()
    s1 = grad_start(1, 2)
    p0 = squares_on(0, q0)

    flying, s1 = grad_on(1, s1)
    x2.wait_send()
    q0.wait_send()
    step1 = squares_in(0, p0)
    x3 = coef_of(3, 1, flying, step1)

    for h in range(2):
        one, two = g_ref[0, h], g_ref[1, h]
        for j in range(own_cols):
            x_v[:, j * patch + h * part : j * patch + (h + 1) * part] = jnp.concatenate(
                [one[j * d : (j + 1) * d], two[j * d : (j + 1) * d]], axis=0
            ).astype(bf)

    def field_of(b):
        field = jnp.zeros((2 * d, patch), f32)
        for j in range(own_cols):
            at = slice(j * patch, (j + 1) * patch)
            field = field + lax.dot_general(
                x_v[:, at], f_v[b, :, at], NT, preferred_element_type=f32
            )
        return field.astype(bf)

    for copy in f_copies + small[2:]:
        copy.wait()
    z_buf[my_r] = field_of(1)
    z = over_row(z_buf, z_buf, z_ss, z_rs, shared=True)
    x3.wait_recv()
    image2 = image_of(3)
    q1 = squares_out(1, image2)

    z.wait_recv()
    fields = [z_buf[r].astype(f32) for r in range(nr)]
    targets = [target_ref[2 * r + 1, my_c] for r in range(nr)]
    for to in range(nc):
        wanted = order_ref[my_r * nc + to]
        mixed = jnp.zeros((2 * d, patch), f32)
        for r in range(nr):
            mixed = mixed + fields[r] * jnp.where(targets[r] == wanted, 1.0, 0.0).astype(f32)
        fc_out[to] = mixed.astype(bf)
    fc = over_col(fc_out, fc_in, fc_ss, fc_rs)
    fc_in[my_c] = fc_out[my_c]

    ev_out[...] = field_of(0)
    odd = my_c % 2
    ev_row = (1 - odd) * ((my_r + nr // 2) % nr) + odd * my_r
    ev = remote(ev_out, ev_in.at[odd], ev_ss, ev_rs.at[odd], ev_row, my_c - odd)
    ev.start()
    p1 = squares_on(1, q1)
    x3.wait_send()
    p0.wait_send()
    for sent in s1:
        sent.wait_send()
    z.wait_send()
    q1.wait_send()
    fc.wait_recv()
    field = fc_in[0].astype(f32)
    for c in range(1, nc):
        field = field + fc_in[c].astype(f32)
    sum_ref[...] = field
    step2 = squares_in(1, p1)
    resid_ref[...] = rhs - step1 * image1 - step2 * image2
    for h in range(2):
        one, two = g_ref[0, h], g_ref[1, h]
        for j in range(own_cols):
            dens_ref[:, j * patch + h * part : j * patch + (h + 1) * part] = (
                step1 * one[j * d : (j + 1) * d] + step2 * two[j * d : (j + 1) * d]
            )

    @pl.when(odd == 0)
    def _():
        for s in range(2):
            remote(ev_out, ev_in.at[s], ev_ss, ev_rs.at[s], my_r, my_c).wait_recv()
        sum_ref[...] += ev_in[0].astype(f32) + ev_in[1].astype(f32)

    field = sum_ref[...]
    far = step1 * field[:d] + step2 * field[d:]
    for row in range(d):
        far_ref[:, row * patch : (row + 1) * patch] = far[row : row + 1]
    ev.wait_send()
    p1.wait_send()
    fc.wait_send()


def hand_on(*refs):
    count = len(refs) // 2
    for n in range(count):
        refs[count + n][...] = refs[n][...]


def per_device(nr, nc, right_side, u_factors, v_factors, ranks, far_blocks, block_target, recv_order):
    dens_count, patch = right_side.shape
    own_rows, all_cols, slot_count, _ = u_factors.shape
    group_rows, own_cols = v_factors.shape[:2]
    block_count, _, unknowns = far_blocks.shape
    recv_total = recv_order.shape[0]
    assert own_rows == 1 and group_rows == nc and all_cols == nc * own_cols
    assert block_count == 2 and recv_total == nr * nc and unknowns == own_cols * patch
    slots = own_cols * slot_count
    rows = own_cols * dens_count
    part = patch // 2
    stages = nr.bit_length() - 1
    assert nr == 1 << stages
    half = -(-slots // (2 * LANES)) * LANES
    bf = jnp.bfloat16
    f32 = jnp.float32
    dma = pltpu.SemaphoreType.DMA
    pair = 2 if nc % 2 == 0 else 1
    u = u_factors.reshape(nc * slots, patch)
    v = v_factors.reshape(nc * slots, patch)
    vmem = pl.BlockSpec(memory_space=pltpu.VMEM)
    hbm = pl.BlockSpec(memory_space=pl.ANY)
    scratch = [
        pltpu.VMEM(right_side.shape, f32),
        pltpu.VMEM(ranks.shape, jnp.int32),
        pltpu.SMEM(block_target.shape, jnp.int32),
        pltpu.SMEM(recv_order.shape, jnp.int32),
        pltpu.VMEM(u.shape, bf),
        pltpu.VMEM(v.shape, bf),
        pltpu.VMEM(far_blocks.shape, bf),
        pltpu.VMEM((2 * dens_count, unknowns), bf),
        pltpu.VMEM((nc // pair, pair * slots), f32),
        pltpu.VMEM((2, 2, rows, part), f32),
        pltpu.VMEM((2 * dens_count, patch), f32),
        pltpu.VMEM((4, nc, 2 * dens_count, half), bf),
        pltpu.VMEM((4, nc, 2 * dens_count, half), bf),
        pltpu.VMEM((2, 2, stages, rows, part), bf),
        pltpu.VMEM((2, 2, stages, rows, part), bf),
        pltpu.VMEM((2, nc, dens_count, LANES), f32),
        pltpu.VMEM((2, nr, dens_count, LANES), f32),
        pltpu.VMEM((nr, 2 * dens_count, patch), bf),
        pltpu.VMEM((nc, 2 * dens_count, patch), bf),
        pltpu.VMEM((nc, 2 * dens_count, patch), bf),
        pltpu.VMEM((2 * dens_count, patch), bf),
        pltpu.VMEM((2, 2 * dens_count, patch), bf),
        dma((4,)), dma((nc // pair,)), dma((nc // pair,)), dma((4,)),
        dma((4,)), dma((4,)),
        dma((2, 2, stages)), dma((2, 2, stages)),
        dma((2,)), dma((2,)),
        dma((2,)), dma((2,)),
        dma, dma,
        dma, dma,
        dma, dma((2,)),
    ]
    matrix = u.size + v.size
    results = pl.pallas_call(
        functools.partial(kernel, nr, nc, dens_count, own_cols, slot_count, patch, pair),
        out_shape=(
            jax.ShapeDtypeStruct((dens_count, unknowns), f32),
            jax.ShapeDtypeStruct((dens_count, patch), f32),
            jax.ShapeDtypeStruct((1, dens_count * patch), f32),
        ),
        in_specs=[hbm] * 7,
        out_specs=(vmem, vmem, vmem),
        scratch_shapes=scratch,
        compiler_params=pltpu.CompilerParams(
            collective_id=0, has_side_effects=True, vmem_limit_bytes=56 * 1024 * 1024
        ),
        cost_estimate=pl.CostEstimate(
            flops=8 * dens_count * matrix + 2 * dens_count * far_blocks.size,
            bytes_accessed=2 * (matrix + far_blocks.size), transcendentals=0,
        ),
    )(right_side, ranks, block_target, recv_order, u, v, far_blocks)
    return pl.pallas_call(
        hand_on,
        out_shape=tuple(jax.ShapeDtypeStruct(x.shape, x.dtype) for x in results),
        in_specs=[vmem] * len(results),
        out_specs=(vmem,) * len(results),
    )(*results)


def solution(mesh):
    return jax.shard_map(
        functools.partial(per_device, mesh.shape["row"], mesh.shape["col"]),
        mesh=mesh,
        in_specs=(
            P(None, ("row", "col")),
            P(("row", "col"), None, None, None),
            P("row", "col", None, None),
            P("row", "col"),
            P("row", None, "col"),
            P(),
            P(),
        ),
        out_specs=(P(None, "col"), P(None, ("row", "col")), P(("row", "col"), None)),
        check_vma=False,
    )
```

```python
import functools

import jax
import jax.numpy as jnp
from jax import lax
from jax.experimental import pallas as pl
from jax.experimental.pallas import tpu as pltpu
from jax.sharding import PartitionSpec as P

MESH = pl.DeviceIdType.MESH
LANES = 128
NT = (((1,), (1,)), ((), ()))
NN = (((1,), (0,)), ((), ()))


def partner_of(me, k, n):
    if n & (n - 1):
        return (me + k) % n
    out = 0
    bit = 1
    while bit < n:
        mine = (me // bit) % 2
        out = out + bit * ((1 - mine) if k & bit else mine)
        bit *= 2
    return out


def kernel(
    nr, nc, dens_count, own_cols, slot_count, patch, pair,
    rhs_hbm, ranks_hbm, target_hbm, order_hbm, u_hbm, v_hbm, f_hbm,
    dens_ref, resid_ref, far_ref,
    rhs_ref, ranks_ref, target_ref, order_ref,
    u_v, v_v, f_v, x_v, kept_ref, g_ref, sum_ref,
    a2a_out, a2a_in, rd_out, rd_in, sc_col, sc_row, z_buf, fc_out, fc_in, ev_out, ev_in,
    small_sem, u_sem, v_sem, f_sem, a2a_ss, a2a_rs, rd_ss, rd_rs,
    scc_ss, scc_rs, scr_ss, scr_rs, z_ss, z_rs, fc_ss, fc_rs, ev_ss, ev_rs,
):
    d = dens_count
    slots = own_cols * slot_count
    half = a2a_out.shape[-1]
    rows = own_cols * d
    groups = nc // pair
    stages = rd_out.shape[2]
    wide = pair * slots
    part = patch // 2
    my_r = lax.axis_index("row")
    my_c = lax.axis_index("col")
    col_peers = [partner_of(my_c, k, nc) for k in range(nc - 1, 0, -1)]
    row_peers = [partner_of(my_r, k, nr) for k in range(nr - 1, 0, -1)]
    bf = jnp.bfloat16
    f32 = jnp.float32

    small = [
        pltpu.make_async_copy(src, dst, small_sem.at[n])
        for n, (src, dst) in enumerate(
            (
                (rhs_hbm, rhs_ref), (ranks_hbm, ranks_ref), (target_hbm, target_ref),
                (order_hbm, order_ref),
            )
        )
    ]
    u_copies, v_copies = [], []
    order = [partner_of(my_c // pair, k, groups) for k in range(groups - 1, -1, -1)]
    for n in range(groups):
        at = pl.ds(pl.multiple_of(order[n] * wide, wide), wide)
        u_copies.append(pltpu.make_async_copy(u_hbm.at[at], u_v.at[at], u_sem.at[n]))
        v_copies.append(pltpu.make_async_copy(v_hbm.at[at], v_v.at[at], v_sem.at[n]))
    f_copies = []
    for b in range(2):
        for h in range(2):
            at = slice(h * part, (h + 1) * part)
            f_copies.append(
                pltpu.make_async_copy(f_hbm.at[b, at], f_v.at[b, at], f_sem.at[2 * b + h])
            )
    for copy in small[:2] + u_copies + small[2:]:
        copy.start()

    barrier = pltpu.get_barrier_semaphore()
    for to in col_peers:
        pl.semaphore_signal(barrier, inc=1, device_id=(my_r, to), device_id_type=MESH)
    for to in row_peers:
        pl.semaphore_signal(barrier, inc=1, device_id=(to, my_c), device_id_type=MESH)

    def remote(src, dst, ssem, rsem, r, c):
        return pltpu.make_async_remote_copy(
            src_ref=src, dst_ref=dst, send_sem=ssem, recv_sem=rsem,
            device_id=(r, c), device_id_type=MESH,
        )

    def over_col(out, into, ssem, rsem, shared=False):
        for to in col_peers:
            src = out.at[my_c] if shared else out.at[to]
            remote(src, into.at[my_c], ssem, rsem, my_r, to).start()
        return remote(out.at[: nc - 1], into.at[: nc - 1], ssem, rsem, my_r, my_c)

    def over_row(out, into, ssem, rsem, shared=False):
        for to in row_peers:
            src = out.at[my_r] if shared else out.at[to]
            remote(src, into.at[my_r], ssem, rsem, to, my_c).start()
        return remote(out.at[: nr - 1], into.at[: nr - 1], ssem, rsem, my_r, my_c)

    def pack(x):
        top, low = x[:, :half], x[:, half:]
        if low.shape[1] < half:
            low = jnp.concatenate([low, jnp.zeros((d, half - low.shape[1]), f32)], axis=1)
        return jnp.concatenate([top, low], axis=0).astype(bf)

    def unpack(x):
        x = x.astype(f32)
        return jnp.concatenate([x[:d], x[d:, : slots - half]], axis=1)

    lane_col = lax.broadcasted_iota(jnp.int32, (d, wide), 1) % slots // slot_count
    diag = jnp.concatenate([(lane_col == j).astype(f32) for j in range(own_cols)], axis=0)

    def put(rnd, q, value):
        for n in range(pair):
            a2a_out[rnd, q * pair + n] = pack(value[:, n * slots : (n + 1) * slots])

    def got(rnd, q):
        return jnp.concatenate([unpack(a2a_in[rnd, q * pair + n]) for n in range(pair)], axis=1)

    def post(rnd, n):
        if n < groups - 1:
            peers = [order[n] * pair + m for m in range(pair)]
        else:
            peers = [my_c // pair * pair + (my_c + m) % pair for m in range(1, pair)]
        for to in peers:
            remote(
                a2a_out.at[rnd, to], a2a_in.at[rnd, my_c], a2a_ss.at[rnd], a2a_rs.at[rnd], my_r, to
            ).start()

    def posted(rnd):
        a2a_in[rnd, my_c] = a2a_out[rnd, my_c]
        return remote(
            a2a_out.at[rnd, : nc - 1], a2a_in.at[rnd, : nc - 1], a2a_ss.at[rnd],
            a2a_rs.at[rnd], my_r, my_c,
        )

    def back_of(rnd, r, first):
        rb = r.astype(bf)
        for n in range(groups):
            if first:
                u_copies[n].wait()
                v_copies[n].start()
            u = u_v[pl.ds(pl.multiple_of(order[n] * wide, wide), wide), :]
            put(rnd, order[n], lax.dot_general(rb, u, NT, preferred_element_type=f32))
            if first and n == 0:
                pl.semaphore_wait(barrier, nc - 1 + nr - 1)
            post(rnd, n)
        return posted(rnd)

    def image_of(rnd):
        image = jnp.zeros((d, patch), f32)
        for q in range(groups):
            u = u_v[q * wide : (q + 1) * wide, :]
            image = image + lax.dot_general(
                got(rnd, q).astype(bf), u, NN, preferred_element_type=f32
            )
        return image

    def grad_start(it, rnd):
        spread = []
        for q in range(groups):
            b = got(rnd, q) * kept_ref[q : q + 1, :]
            spread.append((jnp.concatenate([b] * own_cols, axis=0) * diag).astype(bf))
        sent = []
        for h in range(2):
            acc = jnp.zeros((rows, part), f32)
            for q in range(groups):
                v = v_v[q * wide : (q + 1) * wide, h * part : (h + 1) * part]
                acc = acc + lax.dot_general(spread[q], v, NN, preferred_element_type=f32)
            sent.append(double(it, h, 0, acc))
        return sent

    def double(it, h, stage, value):
        rd_out[it, h, stage] = value.astype(bf)
        copy = remote(
            rd_out.at[it, h, stage], rd_in.at[it, h, stage], rd_ss.at[it, h, stage],
            rd_rs.at[it, h, stage], partner_of(my_r, 1 << stage, nr), my_c,
        )
        copy.start()
        return copy

    def doubled(it, h, stage, copy):
        copy.wait_recv()
        return rd_out[it, h, stage].astype(f32) + rd_in[it, h, stage].astype(f32)

    def grad_on(it, sent):
        flying, done = list(sent), list(sent)
        for stage in range(stages - 1):
            for h in range(2):
                value = doubled(it, h, stage, flying[h])
                flying[h] = double(it, h, stage + 1, value)
                done.append(flying[h])
        return flying, done

    def coef_of(rnd, it, flying, step):
        parts = [jnp.zeros((d, wide), f32)] * groups
        for h in range(2):
            g = doubled(it, h, stages - 1, flying[h])
            if step is not None:
                g = g_ref[0, h] - jnp.concatenate([step] * own_cols, axis=0) * g
            g_ref[it, h] = g
            g = g.astype(bf)
            for n in range(groups):
                at = pl.ds(pl.multiple_of(order[n] * wide, wide), wide)
                v = v_v[at, h * part : (h + 1) * part]
                full = lax.dot_general(g, v, NT, preferred_element_type=f32) * diag
                for j in range(own_cols):
                    parts[n] = parts[n] + full[j * d : (j + 1) * d]
                if h == 1:
                    put(rnd, order[n], parts[n] * kept_ref[pl.ds(order[n], 1), :])
                    post(rnd, n)
        return posted(rnd)

    lane = lax.broadcasted_iota(jnp.int32, (d, LANES), 1)

    def squares_out(it, image):
        squares = jnp.zeros((d, part), f32)
        for h in range(2):
            for j in range(own_cols):
                g = g_ref[it, h, j * d : (j + 1) * d]
                squares = squares + g * g
        grad_sq = jnp.sum(squares, axis=1, keepdims=True) * (1.0 / nr)
        image_sq = jnp.sum(image * image, axis=1, keepdims=True)
        sc_col[it, my_c] = jnp.where(lane < LANES // 2, grad_sq, image_sq)
        return over_col(
            sc_col.at[it], sc_col.at[it], scc_ss.at[it], scc_rs.at[it], shared=True
        )

    def squares_on(it, sent):
        sent.wait_recv()
        total = sc_col[it, 0]
        for c in range(1, nc):
            total = total + sc_col[it, c]
        sc_row[it, my_r] = total
        return over_row(
            sc_row.at[it], sc_row.at[it], scr_ss.at[it], scr_rs.at[it], shared=True
        )

    def squares_in(it, sent):
        sent.wait_recv()
        total = sc_row[it, 0]
        for r in range(1, nr):
            total = total + sc_row[it, r]
        return total[:, :1] / (total[:, LANES // 2 : LANES // 2 + 1] + 1e-6)

    small[1].wait()
    lane_all = lax.broadcasted_iota(jnp.int32, (nc, slots), 1)
    ranks = ranks_ref[...]
    limit = jnp.zeros((nc, slots), jnp.int32)
    for j in range(own_cols):
        limit = jnp.where(lane_all // slot_count == j, ranks[:, j : j + 1], limit)
    kept = (lane_all % slot_count < limit).astype(f32)
    for c in range(nc):
        at = pl.ds(c % pair * slots, slots)
        kept_ref[c // pair : c // pair + 1, at] = kept[c : c + 1]
    small[0].wait()
    rhs = rhs_ref[...]
    x0 = back_of(0, rhs, True)
    for copy in v_copies:
        copy.wait()
    for copy in f_copies[2:] + f_copies[:2]:
        copy.start()
    x0.wait_recv()
    s0 = grad_start(0, 0)
    x0.wait_send()
    flying, s0 = grad_on(0, s0)
    x1 = coef_of(1, 0, flying, None)
    for sent in s0:
        sent.wait_send()
    x1.wait_recv()
    image1 = image_of(1)
    x2 = back_of(2, image1, False)
    q0 = squares_out(0, image1)
    x1.wait_send()
    x2.wait_recv()
    s1 = grad_start(1, 2)
    p0 = squares_on(0, q0)

    flying, s1 = grad_on(1, s1)
    x2.wait_send()
    q0.wait_send()
    step1 = squares_in(0, p0)
    x3 = coef_of(3, 1, flying, step1)

    for h in range(2):
        one, two = g_ref[0, h], g_ref[1, h]
        for j in range(own_cols):
            x_v[:, j * patch + h * part : j * patch + (h + 1) * part] = jnp.concatenate(
                [one[j * d : (j + 1) * d], two[j * d : (j + 1) * d]], axis=0
            ).astype(bf)

    def field_of(b):
        field = lax.dot_general(f_v[b], x_v[...], NT, preferred_element_type=f32)
        return field.T.astype(bf)

    for copy in f_copies + small[2:]:
        copy.wait()
    z_buf[my_r] = field_of(1)
    z = over_row(z_buf, z_buf, z_ss, z_rs, shared=True)
    x3.wait_recv()
    image2 = image_of(3)
    q1 = squares_out(1, image2)

    z.wait_recv()
    fields = [z_buf[r].astype(f32) for r in range(nr)]
    targets = [target_ref[2 * r + 1, my_c] for r in range(nr)]
    for to in range(nc):
        wanted = order_ref[my_r * nc + to]
        mixed = jnp.zeros((2 * d, patch), f32)
        for r in range(nr):
            mixed = mixed + fields[r] * jnp.where(targets[r] == wanted, 1.0, 0.0).astype(f32)
        fc_out[to] = mixed.astype(bf)
    fc = over_col(fc_out, fc_in, fc_ss, fc_rs)
    fc_in[my_c] = fc_out[my_c]

    ev_out[...] = field_of(0)
    odd = my_c % 2
    ev_row = (1 - odd) * ((my_r + nr // 2) % nr) + odd * my_r
    ev = remote(ev_out, ev_in.at[odd], ev_ss, ev_rs.at[odd], ev_row, my_c - odd)
    ev.start()
    p1 = squares_on(1, q1)
    x3.wait_send()
    p0.wait_send()
    for sent in s1:
        sent.wait_send()
    z.wait_send()
    q1.wait_send()
    fc.wait_recv()
    field = fc_in[0].astype(f32)
    for c in range(1, nc):
        field = field + fc_in[c].astype(f32)
    sum_ref[...] = field
    step2 = squares_in(1, p1)
    resid_ref[...] = rhs - step1 * image1 - step2 * image2
    for h in range(2):
        one, two = g_ref[0, h], g_ref[1, h]
        for j in range(own_cols):
            dens_ref[:, j * patch + h * part : j * patch + (h + 1) * part] = (
                step1 * one[j * d : (j + 1) * d] + step2 * two[j * d : (j + 1) * d]
            )

    @pl.when(odd == 0)
    def _():
        for s in range(2):
            remote(ev_out, ev_in.at[s], ev_ss, ev_rs.at[s], my_r, my_c).wait_recv()
        sum_ref[...] += ev_in[0].astype(f32) + ev_in[1].astype(f32)

    field = sum_ref[...]
    far = step1 * field[:d] + step2 * field[d:]
    for row in range(d):
        far_ref[:, row * patch : (row + 1) * patch] = far[row : row + 1]
    ev.wait_send()
    p1.wait_send()
    fc.wait_send()


def hand_on(*refs):
    count = len(refs) // 2
    for n in range(count):
        refs[count + n][...] = refs[n][...]


def per_device(nr, nc, right_side, u_factors, v_factors, ranks, far_blocks, block_target, recv_order):
    dens_count, patch = right_side.shape
    own_rows, all_cols, slot_count, _ = u_factors.shape
    group_rows, own_cols = v_factors.shape[:2]
    block_count, _, unknowns = far_blocks.shape
    recv_total = recv_order.shape[0]
    assert own_rows == 1 and group_rows == nc and all_cols == nc * own_cols
    assert block_count == 2 and recv_total == nr * nc and unknowns == own_cols * patch
    slots = own_cols * slot_count
    rows = own_cols * dens_count
    part = patch // 2
    stages = nr.bit_length() - 1
    assert nr == 1 << stages
    half = -(-slots // (2 * LANES)) * LANES
    bf = jnp.bfloat16
    f32 = jnp.float32
    dma = pltpu.SemaphoreType.DMA
    pair = 2 if nc % 2 == 0 else 1
    u = u_factors.reshape(nc * slots, patch)
    v = v_factors.reshape(nc * slots, patch)
    vmem = pl.BlockSpec(memory_space=pltpu.VMEM)
    hbm = pl.BlockSpec(memory_space=pl.ANY)
    scratch = [
        pltpu.VMEM(right_side.shape, f32),
        pltpu.VMEM(ranks.shape, jnp.int32),
        pltpu.SMEM(block_target.shape, jnp.int32),
        pltpu.SMEM(recv_order.shape, jnp.int32),
        pltpu.VMEM(u.shape, bf),
        pltpu.VMEM(v.shape, bf),
        pltpu.VMEM(far_blocks.shape, bf),
        pltpu.VMEM((2 * dens_count, unknowns), bf),
        pltpu.VMEM((nc // pair, pair * slots), f32),
        pltpu.VMEM((2, 2, rows, part), f32),
        pltpu.VMEM((2 * dens_count, patch), f32),
        pltpu.VMEM((4, nc, 2 * dens_count, half), bf),
        pltpu.VMEM((4, nc, 2 * dens_count, half), bf),
        pltpu.VMEM((2, 2, stages, rows, part), bf),
        pltpu.VMEM((2, 2, stages, rows, part), bf),
        pltpu.VMEM((2, nc, dens_count, LANES), f32),
        pltpu.VMEM((2, nr, dens_count, LANES), f32),
        pltpu.VMEM((nr, 2 * dens_count, patch), bf),
        pltpu.VMEM((nc, 2 * dens_count, patch), bf),
        pltpu.VMEM((nc, 2 * dens_count, patch), bf),
        pltpu.VMEM((2 * dens_count, patch), bf),
        pltpu.VMEM((2, 2 * dens_count, patch), bf),
        dma((4,)), dma((nc // pair,)), dma((nc // pair,)), dma((4,)),
        dma((4,)), dma((4,)),
        dma((2, 2, stages)), dma((2, 2, stages)),
        dma((2,)), dma((2,)),
        dma((2,)), dma((2,)),
        dma, dma,
        dma, dma,
        dma, dma((2,)),
    ]
    matrix = u.size + v.size
    results = pl.pallas_call(
        functools.partial(kernel, nr, nc, dens_count, own_cols, slot_count, patch, pair),
        out_shape=(
            jax.ShapeDtypeStruct((dens_count, unknowns), f32),
            jax.ShapeDtypeStruct((dens_count, patch), f32),
            jax.ShapeDtypeStruct((1, dens_count * patch), f32),
        ),
        in_specs=[hbm] * 7,
        out_specs=(vmem, vmem, vmem),
        scratch_shapes=scratch,
        compiler_params=pltpu.CompilerParams(
            collective_id=0, has_side_effects=True, vmem_limit_bytes=56 * 1024 * 1024
        ),
        cost_estimate=pl.CostEstimate(
            flops=8 * dens_count * matrix + 2 * dens_count * far_blocks.size,
            bytes_accessed=2 * (matrix + far_blocks.size), transcendentals=0,
        ),
    )(right_side, ranks, block_target, recv_order, u, v, far_blocks)
    return pl.pallas_call(
        hand_on,
        out_shape=tuple(jax.ShapeDtypeStruct(x.shape, x.dtype) for x in results),
        in_specs=[vmem] * len(results),
        out_specs=(vmem,) * len(results),
    )(*results)


def solution(mesh):
    return jax.shard_map(
        functools.partial(per_device, mesh.shape["row"], mesh.shape["col"]),
        mesh=mesh,
        in_specs=(
            P(None, ("row", "col")),
            P(("row", "col"), None, None, None),
            P("row", "col", None, None),
            P("row", "col"),
            P("row", None, "col"),
            P(),
            P(),
        ),
        out_specs=(P(None, "col"), P(None, ("row", "col")), P(("row", "col"), None)),
        check_vma=False,
    )
```

```python
import functools

import jax
import jax.numpy as jnp
from jax import lax
from jax.experimental import pallas as pl
from jax.experimental.pallas import tpu as pltpu
from jax.sharding import PartitionSpec as P

MESH = pl.DeviceIdType.MESH
LANES = 128
NT = (((1,), (1,)), ((), ()))
NN = (((1,), (0,)), ((), ()))


def partner_of(me, k, n):
    if n & (n - 1):
        return (me + k) % n
    out = 0
    bit = 1
    while bit < n:
        mine = (me // bit) % 2
        out = out + bit * ((1 - mine) if k & bit else mine)
        bit *= 2
    return out


def kernel(
    nr, nc, dens_count, own_cols, slot_count, patch, pair,
    rhs_hbm, ranks_hbm, target_hbm, order_hbm, u_hbm, v_hbm, f_hbm,
    dens_ref, resid_ref, far_ref,
    rhs_ref, ranks_ref, target_ref, order_ref,
    u_v, v_v, f_v, x_v, kept_ref, g_ref, sum_ref,
    a2a_out, a2a_in, rd_out, rd_in, sc_col, sc_row, z_buf, fc_out, fc_in, ev_out, ev_in,
    small_sem, u_sem, v_sem, f_sem, a2a_ss, a2a_rs, rd_ss, rd_rs,
    scc_ss, scc_rs, scr_ss, scr_rs, z_ss, z_rs, fc_ss, fc_rs, ev_ss, ev_rs,
):
    d = dens_count
    slots = own_cols * slot_count
    half = a2a_out.shape[-1]
    rows = own_cols * d
    groups = nc // pair
    stages = rd_out.shape[2]
    wide = pair * slots
    part = patch // 2
    my_r = lax.axis_index("row")
    my_c = lax.axis_index("col")
    col_peers = [partner_of(my_c, k, nc) for k in range(nc - 1, 0, -1)]
    row_peers = [partner_of(my_r, k, nr) for k in range(nr - 1, 0, -1)]
    bf = jnp.bfloat16
    f32 = jnp.float32

    small = [
        pltpu.make_async_copy(src, dst, small_sem.at[n])
        for n, (src, dst) in enumerate(
            (
                (rhs_hbm, rhs_ref), (ranks_hbm, ranks_ref), (target_hbm, target_ref),
                (order_hbm, order_ref),
            )
        )
    ]
    u_copies, v_copies = [], []
    order = [partner_of(my_c // pair, k, groups) for k in range(groups - 1, -1, -1)]
    for n in range(groups):
        at = pl.ds(pl.multiple_of(order[n] * wide, wide), wide)
        u_copies.append(pltpu.make_async_copy(u_hbm.at[at], u_v.at[at], u_sem.at[n]))
        v_copies.append(pltpu.make_async_copy(v_hbm.at[at], v_v.at[at], v_sem.at[n]))
    f_copies = []
    for b in range(2):
        for h in range(2):
            at = slice(h * part, (h + 1) * part)
            f_copies.append(
                pltpu.make_async_copy(f_hbm.at[b, at], f_v.at[b, at], f_sem.at[2 * b + h])
            )
    for copy in small[:2] + u_copies + small[2:]:
        copy.start()

    barrier = pltpu.get_barrier_semaphore()
    for to in col_peers:
        pl.semaphore_signal(barrier, inc=1, device_id=(my_r, to), device_id_type=MESH)
    for to in row_peers:
        pl.semaphore_signal(barrier, inc=1, device_id=(to, my_c), device_id_type=MESH)

    def remote(src, dst, ssem, rsem, r, c):
        return pltpu.make_async_remote_copy(
            src_ref=src, dst_ref=dst, send_sem=ssem, recv_sem=rsem,
            device_id=(r, c), device_id_type=MESH,
        )

    def over_col(out, into, ssem, rsem, shared=False):
        for to in col_peers:
            src = out.at[my_c] if shared else out.at[to]
            remote(src, into.at[my_c], ssem, rsem, my_r, to).start()
        return remote(out.at[: nc - 1], into.at[: nc - 1], ssem, rsem, my_r, my_c)

    def over_row(out, into, ssem, rsem, shared=False):
        for to in row_peers:
            src = out.at[my_r] if shared else out.at[to]
            remote(src, into.at[my_r], ssem, rsem, to, my_c).start()
        return remote(out.at[: nr - 1], into.at[: nr - 1], ssem, rsem, my_r, my_c)

    def pack(x):
        top, low = x[:, :half], x[:, half:]
        if low.shape[1] < half:
            low = jnp.concatenate([low, jnp.zeros((d, half - low.shape[1]), f32)], axis=1)
        return jnp.concatenate([top, low], axis=0).astype(bf)

    def unpack(x):
        x = x.astype(f32)
        return jnp.concatenate([x[:d], x[d:, : slots - half]], axis=1)

    lane_col = lax.broadcasted_iota(jnp.int32, (d, wide), 1) % slots // slot_count
    diag = jnp.concatenate([(lane_col == j).astype(f32) for j in range(own_cols)], axis=0)

    def put(rnd, q, value):
        for n in range(pair):
            a2a_out[rnd, q * pair + n] = pack(value[:, n * slots : (n + 1) * slots])

    def got(rnd, q):
        return jnp.concatenate([unpack(a2a_in[rnd, q * pair + n]) for n in range(pair)], axis=1)

    def post(rnd, n):
        if n < groups - 1:
            peers = [order[n] * pair + m for m in range(pair)]
        else:
            peers = [my_c // pair * pair + (my_c + m) % pair for m in range(1, pair)]
        for to in peers:
            remote(
                a2a_out.at[rnd, to], a2a_in.at[rnd, my_c], a2a_ss.at[rnd], a2a_rs.at[rnd], my_r, to
            ).start()

    def posted(rnd):
        a2a_in[rnd, my_c] = a2a_out[rnd, my_c]
        return remote(
            a2a_out.at[rnd, : nc - 1], a2a_in.at[rnd, : nc - 1], a2a_ss.at[rnd],
            a2a_rs.at[rnd], my_r, my_c,
        )

    def back_of(rnd, r, first):
        rb = r.astype(bf)
        for n in range(groups):
            if first:
                u_copies[n].wait()
                v_copies[n].start()
            u = u_v[pl.ds(pl.multiple_of(order[n] * wide, wide), wide), :]
            put(rnd, order[n], lax.dot_general(rb, u, NT, preferred_element_type=f32))
            if first and n == 0:
                pl.semaphore_wait(barrier, nc - 1 + nr - 1)
            post(rnd, n)
        return posted(rnd)

    def image_of(rnd):
        image = jnp.zeros((d, patch), f32)
        for q in range(groups):
            u = u_v[q * wide : (q + 1) * wide, :]
            image = image + lax.dot_general(
                got(rnd, q).astype(bf), u, NN, preferred_element_type=f32
            )
        return image

    def grad_start(it, rnd):
        spread = []
        for q in range(groups):
            b = got(rnd, q) * kept_ref[q : q + 1, :]
            spread.append((jnp.concatenate([b] * own_cols, axis=0) * diag).astype(bf))
        sent = []
        for h in range(2):
            acc = jnp.zeros((rows, part), f32)
            for q in range(groups):
                v = v_v[q * wide : (q + 1) * wide, h * part : (h + 1) * part]
                acc = acc + lax.dot_general(spread[q], v, NN, preferred_element_type=f32)
            sent.append(double(it, h, 0, acc))
        return sent

    def double(it, h, stage, value):
        rd_out[it, h, stage] = value.astype(bf)
        copy = remote(
            rd_out.at[it, h, stage], rd_in.at[it, h, stage], rd_ss.at[it, h, stage],
            rd_rs.at[it, h, stage], partner_of(my_r, 1 << stage, nr), my_c,
        )
        copy.start()
        return copy

    def doubled(it, h, stage, copy):
        copy.wait_recv()
        return rd_out[it, h, stage].astype(f32) + rd_in[it, h, stage].astype(f32)

    def grad_on(it, sent):
        flying, done = list(sent), list(sent)
        for stage in range(stages - 1):
            for h in range(2):
                value = doubled(it, h, stage, flying[h])
                flying[h] = double(it, h, stage + 1, value)
                done.append(flying[h])
        return flying, done

    def coef_of(rnd, it, flying, step):
        parts = [jnp.zeros((d, wide), f32)] * groups
        for h in range(2):
            g = doubled(it, h, stages - 1, flying[h])
            if step is not None:
                g = g_ref[0, h] - jnp.concatenate([step] * own_cols, axis=0) * g
            g_ref[it, h] = g
            g = g.astype(bf)
            for n in range(groups):
                at = pl.ds(pl.multiple_of(order[n] * wide, wide), wide)
                v = v_v[at, h * part : (h + 1) * part]
                full = lax.dot_general(g, v, NT, preferred_element_type=f32) * diag
                for j in range(own_cols):
                    parts[n] = parts[n] + full[j * d : (j + 1) * d]
                if h == 1:
                    put(rnd, order[n], parts[n] * kept_ref[pl.ds(order[n], 1), :])
                    post(rnd, n)
        return posted(rnd)

    lane = lax.broadcasted_iota(jnp.int32, (d, LANES), 1)

    def squares_out(it, image):
        squares = jnp.zeros((d, part), f32)
        for h in range(2):
            for j in range(own_cols):
                g = g_ref[it, h, j * d : (j + 1) * d]
                squares = squares + g * g
        grad_sq = jnp.sum(squares, axis=1, keepdims=True) * (1.0 / nr)
        image_sq = jnp.sum(image * image, axis=1, keepdims=True)
        sc_col[it, my_c] = jnp.where(lane < LANES // 2, grad_sq, image_sq)
        return over_col(
            sc_col.at[it], sc_col.at[it], scc_ss.at[it], scc_rs.at[it], shared=True
        )

    def squares_on(it, sent):
        sent.wait_recv()
        total = sc_col[it, 0]
        for c in range(1, nc):
            total = total + sc_col[it, c]
        sc_row[it, my_r] = total
        return over_row(
            sc_row.at[it], sc_row.at[it], scr_ss.at[it], scr_rs.at[it], shared=True
        )

    def squares_in(it, sent):
        sent.wait_recv()
        total = sc_row[it, 0]
        for r in range(1, nr):
            total = total + sc_row[it, r]
        return total[:, :1] / (total[:, LANES // 2 : LANES // 2 + 1] + 1e-6)

    small[1].wait()
    lane_all = lax.broadcasted_iota(jnp.int32, (nc, slots), 1)
    ranks = ranks_ref[...]
    limit = jnp.zeros((nc, slots), jnp.int32)
    for j in range(own_cols):
        limit = jnp.where(lane_all // slot_count == j, ranks[:, j : j + 1], limit)
    kept = (lane_all % slot_count < limit).astype(f32)
    for c in range(nc):
        at = pl.ds(c % pair * slots, slots)
        kept_ref[c // pair : c // pair + 1, at] = kept[c : c + 1]
    small[0].wait()
    rhs = rhs_ref[...]
    x0 = back_of(0, rhs, True)
    for copy in v_copies:
        copy.wait()
    for copy in f_copies[2:] + f_copies[:2]:
        copy.start()
    x0.wait_recv()
    s0 = grad_start(0, 0)
    x0.wait_send()
    flying, s0 = grad_on(0, s0)
    x1 = coef_of(1, 0, flying, None)
    for sent in s0:
        sent.wait_send()
    x1.wait_recv()
    image1 = image_of(1)
    x2 = back_of(2, image1, False)
    q0 = squares_out(0, image1)
    x1.wait_send()
    x2.wait_recv()
    s1 = grad_start(1, 2)
    p0 = squares_on(0, q0)

    flying, s1 = grad_on(1, s1)
    x2.wait_send()
    q0.wait_send()
    step1 = squares_in(0, p0)
    x3 = coef_of(3, 1, flying, step1)

    for h in range(2):
        one, two = g_ref[0, h], g_ref[1, h]
        for j in range(own_cols):
            x_v[:, j * patch + h * part : j * patch + (h + 1) * part] = jnp.concatenate(
                [one[j * d : (j + 1) * d], two[j * d : (j + 1) * d]], axis=0
            ).astype(bf)

    def field_of(b, field, cols):
        for j in cols:
            at = slice(j * patch, (j + 1) * patch)
            field = field + lax.dot_general(
                x_v[:, at], f_v[b, :, at], NT, preferred_element_type=f32
            )
        return field

    for copy in f_copies + small[2:]:
        copy.wait()
    no_field = jnp.zeros((2 * d, patch), f32)
    z_buf[my_r] = field_of(1, no_field, range(own_cols)).astype(bf)
    z = over_row(z_buf, z_buf, z_ss, z_rs, shared=True)
    x3.wait_recv()
    image2 = image_of(3)
    q1 = squares_out(1, image2)

    z.wait_recv()
    fields = [z_buf[r].astype(f32) for r in range(nr)]
    targets = [target_ref[2 * r + 1, my_c] for r in range(nr)]
    for to in range(nc):
        wanted = order_ref[my_r * nc + to]
        mixed = jnp.zeros((2 * d, patch), f32)
        for r in range(nr):
            mixed = mixed + fields[r] * jnp.where(targets[r] == wanted, 1.0, 0.0).astype(f32)
        fc_out[to] = mixed.astype(bf)
    fc = over_col(fc_out, fc_in, fc_ss, fc_rs)
    fc_in[my_c] = fc_out[my_c]

    even = field_of(0, no_field, range(own_cols // 2))
    p1 = squares_on(1, q1)
    even = field_of(0, even, range(own_cols // 2, own_cols))
    ev_out[...] = even.astype(bf)
    odd = my_c % 2
    ev_row = (1 - odd) * ((my_r + nr // 2) % nr) + odd * my_r
    ev = remote(ev_out, ev_in.at[odd], ev_ss, ev_rs.at[odd], ev_row, my_c - odd)
    ev.start()
    x3.wait_send()
    p0.wait_send()
    for sent in s1:
        sent.wait_send()
    z.wait_send()
    q1.wait_send()
    fc.wait_recv()
    field = fc_in[0].astype(f32)
    for c in range(1, nc):
        field = field + fc_in[c].astype(f32)
    sum_ref[...] = field
    step2 = squares_in(1, p1)
    resid_ref[...] = rhs - step1 * image1 - step2 * image2
    for h in range(2):
        one, two = g_ref[0, h], g_ref[1, h]
        for j in range(own_cols):
            dens_ref[:, j * patch + h * part : j * patch + (h + 1) * part] = (
                step1 * one[j * d : (j + 1) * d] + step2 * two[j * d : (j + 1) * d]
            )

    @pl.when(odd == 0)
    def _():
        for s in range(2):
            remote(ev_out, ev_in.at[s], ev_ss, ev_rs.at[s], my_r, my_c).wait_recv()
        sum_ref[...] += ev_in[0].astype(f32) + ev_in[1].astype(f32)

    field = sum_ref[...]
    far = step1 * field[:d] + step2 * field[d:]
    for row in range(d):
        far_ref[:, row * patch : (row + 1) * patch] = far[row : row + 1]
    ev.wait_send()
    p1.wait_send()
    fc.wait_send()


def hand_on(*refs):
    count = len(refs) // 2
    for n in range(count):
        refs[count + n][...] = refs[n][...]


def per_device(nr, nc, right_side, u_factors, v_factors, ranks, far_blocks, block_target, recv_order):
    dens_count, patch = right_side.shape
    own_rows, all_cols, slot_count, _ = u_factors.shape
    group_rows, own_cols = v_factors.shape[:2]
    block_count, _, unknowns = far_blocks.shape
    recv_total = recv_order.shape[0]
    assert own_rows == 1 and group_rows == nc and all_cols == nc * own_cols
    assert block_count == 2 and recv_total == nr * nc and unknowns == own_cols * patch
    slots = own_cols * slot_count
    rows = own_cols * dens_count
    part = patch // 2
    stages = nr.bit_length() - 1
    assert nr == 1 << stages
    half = -(-slots // (2 * LANES)) * LANES
    bf = jnp.bfloat16
    f32 = jnp.float32
    dma = pltpu.SemaphoreType.DMA
    pair = 2 if nc % 2 == 0 else 1
    u = u_factors.reshape(nc * slots, patch)
    v = v_factors.reshape(nc * slots, patch)
    vmem = pl.BlockSpec(memory_space=pltpu.VMEM)
    hbm = pl.BlockSpec(memory_space=pl.ANY)
    scratch = [
        pltpu.VMEM(right_side.shape, f32),
        pltpu.VMEM(ranks.shape, jnp.int32),
        pltpu.SMEM(block_target.shape, jnp.int32),
        pltpu.SMEM(recv_order.shape, jnp.int32),
        pltpu.VMEM(u.shape, bf),
        pltpu.VMEM(v.shape, bf),
        pltpu.VMEM(far_blocks.shape, bf),
        pltpu.VMEM((2 * dens_count, unknowns), bf),
        pltpu.VMEM((nc // pair, pair * slots), f32),
        pltpu.VMEM((2, 2, rows, part), f32),
        pltpu.VMEM((2 * dens_count, patch), f32),
        pltpu.VMEM((4, nc, 2 * dens_count, half), bf),
        pltpu.VMEM((4, nc, 2 * dens_count, half), bf),
        pltpu.VMEM((2, 2, stages, rows, part), bf),
        pltpu.VMEM((2, 2, stages, rows, part), bf),
        pltpu.VMEM((2, nc, dens_count, LANES), f32),
        pltpu.VMEM((2, nr, dens_count, LANES), f32),
        pltpu.VMEM((nr, 2 * dens_count, patch), bf),
        pltpu.VMEM((nc, 2 * dens_count, patch), bf),
        pltpu.VMEM((nc, 2 * dens_count, patch), bf),
        pltpu.VMEM((2 * dens_count, patch), bf),
        pltpu.VMEM((2, 2 * dens_count, patch), bf),
        dma((4,)), dma((nc // pair,)), dma((nc // pair,)), dma((4,)),
        dma((4,)), dma((4,)),
        dma((2, 2, stages)), dma((2, 2, stages)),
        dma((2,)), dma((2,)),
        dma((2,)), dma((2,)),
        dma, dma,
        dma, dma,
        dma, dma((2,)),
    ]
    matrix = u.size + v.size
    results = pl.pallas_call(
        functools.partial(kernel, nr, nc, dens_count, own_cols, slot_count, patch, pair),
        out_shape=(
            jax.ShapeDtypeStruct((dens_count, unknowns), f32),
            jax.ShapeDtypeStruct((dens_count, patch), f32),
            jax.ShapeDtypeStruct((1, dens_count * patch), f32),
        ),
        in_specs=[hbm] * 7,
        out_specs=(vmem, vmem, vmem),
        scratch_shapes=scratch,
        compiler_params=pltpu.CompilerParams(
            collective_id=0, has_side_effects=True, vmem_limit_bytes=56 * 1024 * 1024
        ),
        cost_estimate=pl.CostEstimate(
            flops=8 * dens_count * matrix + 2 * dens_count * far_blocks.size,
            bytes_accessed=2 * (matrix + far_blocks.size), transcendentals=0,
        ),
    )(right_side, ranks, block_target, recv_order, u, v, far_blocks)
    return pl.pallas_call(
        hand_on,
        out_shape=tuple(jax.ShapeDtypeStruct(x.shape, x.dtype) for x in results),
        in_specs=[vmem] * len(results),
        out_specs=(vmem,) * len(results),
    )(*results)


def solution(mesh):
    return jax.shard_map(
        functools.partial(per_device, mesh.shape["row"], mesh.shape["col"]),
        mesh=mesh,
        in_specs=(
            P(None, ("row", "col")),
            P(("row", "col"), None, None, None),
            P("row", "col", None, None),
            P("row", "col"),
            P("row", None, "col"),
            P(),
            P(),
        ),
        out_specs=(P(None, "col"), P(None, ("row", "col")), P(("row", "col"), None)),
        check_vma=False,
    )
```
